256 devices in a mesh: dp: 8 (over x, core), seq: 32 (over z, y).
Axes of the slice: x: 4, y: 4, z: 8, core: 2. Of those that a mesh axis runs over, the one named last changes fastest.
Arguments:
- spatial_qkv: bfloat16 [8, 32, 128, 3456], P('dp', 'seq')
- lengths: int32 [8], P('dp'), may hold values from 4 to 32, as said below
- w_qkv: bfloat16 [1152, 3456], P('seq'), may hold values from -0.75 to 0.75
- cotangent: bfloat16 [8, 32, 128, 1152], P('dp', 'seq'), may hold values from -6 to 6
Outputs:
- block_out: bfloat16 [8, 32, 128, 1152], P('dp', 'seq')
- grad_qkv: bfloat16 [8, 32, 128, 3456], P('dp', 'seq')
- grad_w: bfloat16 [1152, 3456], P('seq', 'dp')
The draws below stay inside these ranges and needn't reach their ends.
Inputs may be any that keep to these rules, and one draw needn't show every extreme that they name: `lengths`: every video has at least one live frame, and some video fills all 32 slots.
All inputs are finite; a program needn't handle non-finite values.
Results may differ from the reference program's by a relative error of at most 0.035.
The reference program's roundings to bfloat16 on the way count: a program that leaves them out, or rounds other values in their place, can miss the bound.
Values may be sent and summed in bfloat16 or wider, within the bound.
A program may use at most 128 MiB of HBM per device.

```python
import jax
import jax.numpy as jnp
from jax import lax

D = 1152
HEADS = 16
PATCH_DEV = 4
FRAMES = 32
PATCHES = 128
VIDEOS = 8


def draw_spatial_qkv(key, part):
    key = jax.random.fold_in(key, 2)
    shape = (VIDEOS, FRAMES, PATCHES, 3 * D)
    return jax.random.normal(key, shape, jnp.float32).astype(jnp.bfloat16)


def draw_lengths(key, part):
    key = jax.random.fold_in(key, 1)
    first_key, second_key = jax.random.split(key)
    drawn = jax.random.randint(first_key, (VIDEOS,), max(1, FRAMES // 8), FRAMES + 1)
    chosen = jax.random.randint(second_key, (), 0, VIDEOS)
    return jnp.where(jnp.arange(VIDEOS) == chosen, FRAMES, drawn).astype(jnp.int32)


def level_of(stream_key, dims, shards, smallest, high):
    gain, own = 1.0, jax.random.fold_in(stream_key, 6)
    for axis_at, parts in shards:
        heights = jnp.exp(jax.random.uniform(jax.random.fold_in(own, axis_at), (parts,), jnp.float32, smallest / len(shards), high / len(shards)))
        gain = gain * jnp.repeat(heights, dims[axis_at] // parts).reshape([-1 if axis == axis_at else 1 for axis in range(len(dims))])
    return gain


def scatter_about(own_key, extent, deviation, limit, cuts=(), kind=jnp.bfloat16):
    result = jax.random.normal(own_key, extent, jnp.float32) * deviation
    if len(cuts) > 0:
        result = level_of(own_key, extent, cuts, -0.22, 0.18) * result
    return jnp.clip(result, min=-limit, max=limit).astype(kind)


def setup_inputs(seed: int = 0) -> dict:
    keys = jax.random.split(jax.random.key(seed), 5)
    spatial_qkv = draw_spatial_qkv(jax.random.fold_in(keys[4], 71), 0)
    lengths = draw_lengths(jax.random.fold_in(keys[4], 71), 0)
    w_qkv = scatter_about(keys[2], (D, 3 * D), (D // 16) ** -0.5, 0.75, ((0, 32),))
    cotangent = scatter_about(keys[3], (VIDEOS, FRAMES, PATCHES, D), 1.0, 6.0, ((0, 8), (1, 32)))
    return dict(spatial_qkv=spatial_qkv, lengths=lengths, w_qkv=w_qkv, cotangent=cotangent)


SPATIAL_LAYOUTS = ("blhe,bmhe->bhlm", "bhlm,bmhe->blhe", "bhlm,blhe->bmhe")
TEMPORAL_FORMS = ("lbhe,mbhe->bhlm", "bhlm,mbhe->lbhe", "bhlm,lbhe->mbhe")


def split_heads(array, head_count):
    return array.reshape(array.shape[:-1] + (head_count, array.shape[-1] // head_count))


def join_heads(array):
    return array.reshape(array.shape[:-2] + (array.shape[-2] * array.shape[-1],))


def attend_forward(queries, keys_in, values_in, key_live, forms, head_count):
    scale = (queries.shape[-1] // head_count) ** -0.5
    query_heads = split_heads(queries, head_count).astype(jnp.float32)
    key_heads = split_heads(keys_in, head_count).astype(jnp.float32)
    value_heads = split_heads(values_in, head_count).astype(jnp.float32)
    scores = jnp.einsum(forms[0], query_heads, key_heads) * scale
    if key_live is not None:
        scores = jnp.where(key_live, scores, -1e30)
    peak = jnp.max(scores, axis=-1, keepdims=True)
    expo = jnp.exp(scores - peak)
    probs = expo / jnp.sum(expo, axis=-1, keepdims=True)
    probs_low = probs.astype(jnp.bfloat16)
    output = jnp.einsum(forms[1], probs_low.astype(jnp.float32), value_heads)
    return join_heads(output), probs, probs_low


def attend_backward(grad_out, queries, keys_in, values_in, probs, probs_low, forms, head_count):
    scale = (queries.shape[-1] // head_count) ** -0.5
    grad_heads = split_heads(grad_out, head_count).astype(jnp.float32)
    query_heads = split_heads(queries, head_count).astype(jnp.float32)
    key_heads = split_heads(keys_in, head_count).astype(jnp.float32)
    value_heads = split_heads(values_in, head_count).astype(jnp.float32)
    grad_values = jnp.einsum(forms[2], probs_low.astype(jnp.float32), grad_heads)
    grad_probs = jnp.einsum(forms[0], grad_heads, value_heads)
    grad_scores = probs * (grad_probs - jnp.sum(grad_probs * probs, axis=-1, keepdims=True))
    scaled_low = (grad_scores * scale).astype(jnp.bfloat16).astype(jnp.float32)
    grad_queries = jnp.einsum(forms[1], scaled_low, key_heads)
    grad_keys = jnp.einsum(forms[2], scaled_low, query_heads)
    return jnp.concatenate([join_heads(grad_queries), join_heads(grad_keys), join_heads(grad_values)], axis=-1)


def group_terms(spatial_out, grad_projected, start):
    model_width = spatial_out.shape[-1]
    group_count = PATCHES // PATCH_DEV
    act_groups = jnp.moveaxis(spatial_out.reshape(FRAMES, group_count, PATCH_DEV, model_width), 1, 0)
    grad_groups = jnp.moveaxis(grad_projected.reshape(FRAMES, group_count, PATCH_DEV, 3 * model_width), 1, 0)

    def add_group(total, pair):
        act_block, grad_block = pair
        term = jnp.dot(act_block.reshape(-1, model_width).T, grad_block.reshape(-1, 3 * model_width),
                       preferred_element_type=jnp.float32)
        term_low = lax.optimization_barrier(term.astype(jnp.bfloat16))
        return total + term_low.astype(jnp.float32), None

    total, unused = lax.scan(add_group, start, (act_groups, grad_groups))
    return total


def one_video(packed_tensor, length, weight, grad_in, running):
    model_width = weight.shape[0]
    spatial_out, spatial_weights, spatial_reduced = attend_forward(
        packed_tensor[..., :model_width], packed_tensor[..., model_width:2 * model_width], packed_tensor[..., 2 * model_width:], None, SPATIAL_LAYOUTS, HEADS)
    spatial_out = spatial_out.astype(jnp.bfloat16)
    projected = jnp.dot(spatial_out.reshape(-1, model_width), weight, preferred_element_type=jnp.float32)
    projected = projected.astype(jnp.bfloat16).reshape(FRAMES, PATCHES, 3 * model_width)
    key_live = (jnp.arange(FRAMES) < length).reshape(1, 1, 1, FRAMES)
    tqueries = projected[..., :model_width]
    tkeys = projected[..., model_width:2 * model_width]
    tvalues = projected[..., 2 * model_width:]
    temporal_out, temporal_probs, temporal_low = attend_forward(tqueries, tkeys, tvalues, key_live, TEMPORAL_FORMS, HEADS)
    temporal_out = temporal_out.astype(jnp.bfloat16)
    block_out = (spatial_out.astype(jnp.float32) + temporal_out.astype(jnp.float32)).astype(jnp.bfloat16)
    grad_projected = attend_backward(grad_in, tqueries, tkeys, tvalues, temporal_probs, temporal_low,
                                     TEMPORAL_FORMS, HEADS).astype(jnp.bfloat16)
    grad_rows = grad_projected.reshape(-1, 3 * model_width)
    back_term = jnp.dot(grad_rows, weight.T, preferred_element_type=jnp.float32).reshape(FRAMES, PATCHES, model_width)
    spatial_gradient = (grad_in.astype(jnp.float32) + back_term).astype(jnp.bfloat16)
    running = group_terms(spatial_out, grad_projected, running)
    grad_packed = attend_backward(spatial_gradient, packed_tensor[..., :model_width], packed_tensor[..., model_width:2 * model_width],
                                  packed_tensor[..., 2 * model_width:], spatial_weights, spatial_reduced, SPATIAL_LAYOUTS, HEADS)
    return block_out, grad_packed.astype(jnp.bfloat16), running


def reference(spatial_qkv, lengths, w_qkv, cotangent):
    def step(carry, inputs):
        packed_tensor, length, grad_in = inputs
        block_out, grad_packed, carry = one_video(packed_tensor, length, w_qkv, grad_in, carry)
        return carry, (block_out, grad_packed)

    start = jnp.zeros(w_qkv.shape, jnp.float32)
    total, outputs = lax.scan(step, start, (spatial_qkv, lengths, cotangent))
    return outputs[0], outputs[1], total.astype(jnp.bfloat16)
```

```python
import jax
import jax.numpy as jnp
from jax import lax
from jax.experimental import pallas as pl
from jax.experimental.pallas import tpu as pltpu
from jax.sharding import PartitionSpec as P

HEADS = 16
WIDTH = 1152
HEAD = 72
NY, NZ, NX, NC = 4, 8, 4, 2
MESH = pl.DeviceIdType.MESH
F32, BF16 = jnp.float32, jnp.bfloat16
SCALE = HEAD ** (-0.5)


def dot(a, b):
    return lax.dot_general(a, b, (((1,), (0,)), ((), ())), preferred_element_type=F32)


def dot_nt(a, b):
    return lax.dot_general(a, b, (((1,), (1,)), ((), ())), preferred_element_type=F32)


def dot_tn(a, b):
    return lax.dot_general(a, b, (((0,), (0,)), ((), ())), preferred_element_type=F32)


def half(window, j):
    return window[:, 0:256] if j < 2 else window[:, 128:384]


def head_masks(off):
    lane = lax.broadcasted_iota(jnp.int32, (128, 256), 1)
    masks = []
    for j in range(4):
        low = off + HEAD * j - (128 if j >= 2 else 0)
        masks.append(jnp.where((lane >= low) & (lane < low + HEAD), 1.0, 0.0).astype(BF16))
    return masks


def join(parts):
    left, right = parts[0] + parts[1], parts[2] + parts[3]
    return jnp.concatenate(
        [left[:, 0:128], left[:, 128:256] + right[:, 0:128], right[:, 128:256]], axis=1
    )


def forward4(q, k, v, masks, live):
    probs, outs = [], []
    for j in range(4):
        scores = dot_nt(half(q, j) * masks[j], half(k, j)) * SCALE
        if live is not None:
            scores = jnp.where(live, scores, -1e30)
        expo = jnp.exp(scores - jnp.max(scores, axis=-1, keepdims=True))
        prob = expo * (1.0 / jnp.sum(expo, axis=-1, keepdims=True))
        probs.append(prob)
        outs.append(dot(prob.astype(BF16), half(v, j) * masks[j]))
    return join(outs), probs


def backward4(g, q, k, v, probs, masks):
    dqs, dks, dvs = [], [], []
    for j in range(4):
        prob = probs[j]
        gh = half(g, j) * masks[j]
        dvs.append(dot_tn(prob.astype(BF16), gh))
        gp = dot_nt(gh, half(v, j))
        gs = prob * (gp - jnp.sum(gp * prob, axis=-1, keepdims=True))
        low = (gs * SCALE).astype(BF16)
        dqs.append(dot(low, half(k, j) * masks[j]))
        dks.append(dot_tn(low, half(q, j) * masks[j]))
    return join(dqs), join(dks), join(dvs)


def remote(src, dst, ssem, rsem, dp, s):
    return pltpu.make_async_remote_copy(
        src_ref=src, dst_ref=dst, send_sem=ssem, recv_sem=rsem,
        device_id=(dp, s), device_id_type=MESH,
    )


def m16(value):
    return pl.multiple_of(value, 16)


def kernel(
    len_ref, qkv, w, cot, bo, gqkv, gw,
    acc, prs, sob, wp, wr, wm, wf, so, cy, cz, c32, pj, to32, tob, ty, tf, gp32, gpb,
    gs, gr, gz, gf, pw, crv, kr, xr, zr, zb, fr, fs, fy, fd, gwf,
    wy_s, wy_r, wzr_s, wzr_r, wzl_s, wzl_r, wd_s, wd_r, cy_s, cy_r, cz_s, cz_r,
    sz_s, sz_r, sy_s, sy_r, ty_s, ty_r, tz_s, tz_r, gy_s, gy_r, gz_s, gz_r,
    pc_s, pc_r, px_s, px_r, pz_s, pz_r, py_s, py_r, pd_s, pd_r,
):
    dp, s = lax.axis_index("dp"), lax.axis_index("seq")
    y, z = lax.rem(s, NY), lax.div(s, NY)
    c, x = lax.rem(dp, NC), lax.div(dp, NC)
    sib = x * NC + (1 - c)
    sent = []

    def at_y(k):
        return lax.rem(y + k + NY, NY)

    def at_z(k):
        return lax.rem(z + k + NZ, NZ)

    def at_x(k):
        return lax.rem(x + k + NX, NX)

    def send(src, dst, ssem, rsem, dp_to, s_to):
        copy = remote(src, dst, ssem, rsem, dp_to, s_to)
        copy.start()
        sent.append(copy)

    def arrived(dst, ssem, rsem):
        remote(dst, dst, ssem, rsem, dp, s).wait_recv()

    barrier = pltpu.get_barrier_semaphore()
    for k in range(1, NY):
        pl.semaphore_signal(barrier, inc=1, device_id=(dp, z * NY + at_y(k)), device_id_type=MESH)
    for k in range(1, NZ):
        pl.semaphore_signal(barrier, inc=1, device_id=(dp, at_z(k) * NY + y), device_id_type=MESH)
    for k in range(1, NX * NC):
        pl.semaphore_signal(
            barrier, inc=1, device_id=(lax.rem(dp + k, NX * NC), s), device_id_type=MESH
        )

    wrow = w[...].astype(F32)
    for g in range(NY):
        piece = jnp.concatenate(
            [wrow[:, 288 * g + WIDTH * i: 288 * g + WIDTH * i + 288] for i in range(3)]
            + [jnp.zeros((36, 160), F32)], axis=1
        )
        piece = jnp.concatenate([piece, jnp.zeros((12, 1024), F32)], axis=0).astype(BF16)
        wp[g, 0] = piece[:, 0:512]
        wp[g, 1] = piece[:, 512:1024]
    cy[y] = cot[:, pl.ds(pl.multiple_of(256 * y, 128), 384)]
    wr[y] = wp[y, c]

    pl.semaphore_wait(barrier, NY + NZ + NX * NC - 3)
    for k in range(1, NY):
        to = at_y(k)
        send(wp.at[to, c], wr.at[y], wy_s.at[k - 1], wy_r.at[k - 1], dp, z * NY + to)
    for k in range(1, NY):
        to = at_y(k)
        send(
            cot.at[:, pl.ds(pl.multiple_of(256 * to, 128), 384)], cy.at[y],
            cy_s.at[k - 1], cy_r.at[k - 1], dp, z * NY + to,
        )

    acc[...] = jnp.zeros_like(acc)

    def spatial_forward(group):
        at = pl.multiple_of(256 * group, 128)
        q, k, v = (qkv[:, pl.ds(at + WIDTH * i, 384)] for i in range(3))
        out, probs = forward4(q, k, v, head_masks(32 * group), None)
        acc[:, pl.ds(at, 384)] += out
        for j in range(4):
            prs[4 * group + j] = probs[j]

    def block(k):
        return wf.at[c, pl.ds(m16(144 * at_z(k)), 144)]

    def to_sibling(k, order):
        send(block(k), block(k), wd_s.at[order], wd_r.at[order], sib, s)

    def ring(step):
        if step > 0:
            arrived(block(-step), wzr_s.at[step - 1], wzr_r.at[step - 1])
        if step < 4:
            send(block(-step), block(-step), wzr_s.at[step], wzr_r.at[step], dp, at_z(1) * NY + y)
        if 0 < step < 4:
            arrived(block(step), wzl_s.at[step - 1], wzl_r.at[step - 1])
        if step < 3:
            send(block(step), block(step), wzl_s.at[step], wzl_r.at[step], dp, at_z(-1) * NY + y)
        to_sibling(-step, step)
        if 0 < step < 4:
            to_sibling(step, 4 + step)

    spatial_forward(0)
    for k in range(1, NY):
        arrived(wr.at[at_y(-k)], wy_s.at[k - 1], wy_r.at[k - 1])
    for i in range(NY):
        wm[36 * i: 36 * i + 48, :] = wr[i].astype(F32)
    wf[c, pl.ds(m16(144 * z), 144)] = wm[0:144, :].astype(BF16)
    ring(0)
    spatial_forward(1)
    ring(1)
    spatial_forward(2)
    spatial_forward(3)
    ring(2)
    sob[...] = acc[:, 0:WIDTH].astype(BF16)
    for k in range(1, NZ):
        to = at_z(k)
        send(
            sob.at[pl.ds(m16(16 * to), 16)], so.at[z, y],
            sz_s.at[k - 1], sz_r.at[k - 1], dp, to * NY + y,
        )
    so[z, y] = sob[pl.ds(m16(16 * z), 16), :]
    for k in range(1, NY):
        arrived(cy.at[at_y(-k)], cy_s.at[k - 1], cy_r.at[k - 1])
    for k in range(1, NZ):
        to = at_z(k)
        send(
            cy.at[:, pl.ds(m16(16 * to), 16)], cz.at[z],
            cz_s.at[k - 1], cz_r.at[k - 1], dp, to * NY + y,
        )
    cz[z] = cy[:, pl.ds(m16(16 * z), 16), :]
    ring(3)
    for k in range(1, NZ):
        arrived(so.at[at_z(-k), y], sz_s.at[k - 1], sz_r.at[k - 1])
    for k in range(1, NY):
        to = at_y(k)
        send(so.at[:, y], so.at[:, y], sy_s.at[k - 1], sy_r.at[k - 1], dp, z * NY + to)
    ring(4)
    other = 1 - c
    for order, k in enumerate((0, -1, -2, -3, -4, 1, 2, 3)):
        arrived(
            wf.at[other, pl.ds(m16(144 * at_z(k)), 144)], wd_s.at[order], wd_r.at[order]
        )

    def project(at):
        rows = so[:, at].reshape(128, WIDTH)
        first = dot(rows, wf[0])
        second = dot(rows, wf[1, :, 0:384])
        for i in range(NZ):
            place = pl.ds(m16((NY * i + at) * 16), 16)
            for t in range(4):
                pj[t, place] = first[16 * i: 16 * i + 16, 128 * t: 128 * t + 128]
            for t in range(3):
                pj[4 + t, place] = second[16 * i: 16 * i + 16, 128 * t: 128 * t + 128]

    project(y)
    for k in range(1, NY):
        arrived(so.at[:, at_y(-k)], sy_s.at[k - 1], sy_r.at[k - 1])
        project(at_y(-k))

    for k in range(1, NZ):
        arrived(cz.at[at_z(-k)], cz_s.at[k - 1], cz_r.at[k - 1])
    g_in = cz[...].reshape(512, 384).astype(F32)
    turned = g_in
    for k in range(1, NY):
        turned = jnp.where(y == k, pltpu.roll(g_in, 384 - 32 * k, 1), turned)
    for t in range(3):
        c32[t] = turned[:, 128 * t: 128 * t + 128]

    length = len_ref[0]
    row = lax.broadcasted_iota(jnp.int32, (128, 128), 0)
    col = lax.broadcasted_iota(jnp.int32, (128, 128), 1)
    live = ((row >> 5) == (col >> 5)) & ((col & 31) < length)
    masks = head_masks(0)

    def temporal(b, carry):
        def rows_of(ref, first):
            return jnp.concatenate(
                [
                    jnp.concatenate(
                        [ref[t, pl.ds(4 * b + i, 32, stride=16), :] for i in range(4)], axis=0
                    )
                    for t in range(first, first + 3)
                ],
                axis=1,
            )

        q = rows_of(pj, 0).astype(BF16)
        k = pltpu.roll(rows_of(pj, 2), 384 - 32, 1).astype(BF16)
        v = pltpu.roll(rows_of(pj, 4), 384 - 64, 1).astype(BF16)
        g = rows_of(c32, 0).astype(BF16)
        out, probs = forward4(q, k, v, masks, live)
        dq, dk, dv = backward4(g, q, k, v, probs, masks)
        dk, dv = pltpu.roll(dk, 32, 1), pltpu.roll(dv, 64, 1)
        packed = jnp.concatenate(
            [dq[:, 0:256], dq[:, 256:384] + dk[:, 0:128], dk[:, 128:256],
             dk[:, 256:384] + dv[:, 0:128], dv[:, 128:384]], axis=1
        )
        for i in range(4):
            place = pl.ds(4 * b + i, 32, stride=16)
            for t in range(3):
                to32[t, place, :] = out[32 * i: 32 * i + 32, 128 * t: 128 * t + 128]
            for t in range(7):
                gp32[t, place, :] = packed[32 * i: 32 * i + 32, 128 * t: 128 * t + 128]
        return carry

    lax.fori_loop(0, 4, temporal, 0)

    for t in range(7):
        gpb[:, :, :, 128 * t: 128 * t + 128] = gp32[t].astype(BF16).reshape(NZ, NY, 16, 128)
    gpb[:, :, :, 896:1024] = jnp.zeros((NZ, NY, 16, 128), BF16)

    def back(to):
        rows = gpb[:, to].reshape(128, 1024)
        part = dot_nt(rows[:, 0:512], wf[0]) + dot_nt(rows[:, 512:896], wf[1, :, 0:384])
        gs[to] = part.astype(BF16).reshape(NZ, 16, WIDTH)

    for k in range(1, NY):
        to = at_y(k)
        back(to)
        send(gs.at[to], gr.at[k - 1], gy_s.at[k - 1], gy_r.at[k - 1], dp, z * NY + to)
    back(y)

    t_out = jnp.concatenate([to32[t] for t in range(3)], axis=1)
    turned = t_out
    for k in range(1, NY):
        turned = jnp.where(y == k, pltpu.roll(t_out, 32 * k, 1), turned)
    tob[...] = turned.astype(BF16).reshape(NZ, NY, 16, 384)
    for k in range(1, NY):
        to = at_y(k)
        send(tob.at[:, to], ty.at[y], ty_s.at[k - 1], ty_r.at[k - 1], dp, z * NY + to)
    ty[y] = tob[:, y]

    def weight_chunk(i, carry):
        at = pl.multiple_of(128 * i, 128)
        part = dot_tn(
            so[:, :, :, pl.ds(at, 128)].reshape(512, 128), gpb[...].reshape(512, 1024)
        ).astype(BF16)
        pw[0, pl.ds(at, 128)] = part[:, 0:512]
        pw[1, pl.ds(at, 128)] = part[:, 512:1024]
        return carry

    lax.fori_loop(0, 9, weight_chunk, 0)
    send(pw.at[1 - c], crv, pc_s, pc_r, sib, s)

    for k in range(1, NY):
        arrived(gr.at[k - 1], gy_s.at[k - 1], gy_r.at[k - 1])
    total = gs[y].astype(F32)
    for k in range(1, NY):
        total = total + gr[k - 1].astype(F32)
    gz[...] = total.astype(BF16)
    for k in range(1, NZ):
        to = at_z(k)
        send(gz.at[to], gf.at[z], gz_s.at[k - 1], gz_r.at[k - 1], dp, to * NY + y)
    gf[z] = gz[z]

    arrived(crv, pc_s, pc_r)
    kr[...] = (pw[c].astype(F32) + crv[...].astype(F32)).astype(BF16)
    for k in range(1, NX):
        to = at_x(k)
        send(
            kr.at[:, pl.ds(pl.multiple_of(128 * to, 128), 128)], xr.at[k - 1],
            px_s.at[k - 1], px_r.at[k - 1], to * NC + c, s,
        )

    for k in range(1, NY):
        arrived(ty.at[at_y(-k)], ty_s.at[k - 1], ty_r.at[k - 1])
    for k in range(1, NZ):
        to = at_z(k)
        send(ty.at[:, to], tf.at[z], tz_s.at[k - 1], tz_r.at[k - 1], dp, to * NY + y)
    tf[z] = ty[:, z]

    for k in range(1, NZ):
        arrived(gf.at[at_z(-k)], gz_s.at[k - 1], gz_r.at[k - 1])
    grad = (cot[...].astype(F32) + gf[...].reshape(128, WIDTH).astype(F32)).astype(BF16)
    sob2 = grad
    gf[...] = sob2.reshape(NZ, 16, WIDTH)
    acc[...] = jnp.zeros_like(acc)

    def spatial_backward(group, carry):
        at = pl.multiple_of(256 * group, 128)
        q, k, v = (qkv[:, pl.ds(at + WIDTH * i, 384)] for i in range(3))
        g = gf[:, :, pl.ds(at, 384)].reshape(128, 384)
        probs = [prs[4 * group + j] for j in range(4)]
        grads = backward4(g, q, k, v, probs, head_masks(32 * group))
        for i in range(3):
            acc[:, pl.ds(at + WIDTH * i, 384)] += grads[i]
        return carry

    lax.fori_loop(0, 2, spatial_backward, 0)

    for k in range(1, NX):
        arrived(xr.at[k - 1], px_s.at[k - 1], px_r.at[k - 1])
    total = kr[:, pl.ds(pl.multiple_of(128 * x, 128), 128)].astype(F32)
    for k in range(1, NX):
        total = total + xr[k - 1].astype(F32)
    zr[...] = total.astype(BF16).reshape(NZ, 144, 128)
    for k in range(1, NZ):
        to = at_z(k)
        send(zr.at[to], zb.at[z], pz_s.at[k - 1], pz_r.at[k - 1], dp, to * NY + y)
    zb[z] = zr[z]

    lax.fori_loop(2, 4, spatial_backward, 0)

    for k in range(1, NZ):
        arrived(zb.at[at_z(-k)], pz_s.at[k - 1], pz_r.at[k - 1])
    total = zb[0].astype(F32)
    for i in range(1, NZ):
        total = total + zb[i].astype(F32)
    fr[0:144, :] = total
    fr[144:160, :] = jnp.zeros((16, 128), F32)
    for i in range(NY):
        fs[i] = fr[36 * i: 36 * i + 48, :].astype(BF16)
    for k in range(1, NY):
        to = at_y(k)
        send(fs.at[to], fy.at[y], py_s.at[k - 1], py_r.at[k - 1], dp, z * NY + to)
    fy[y] = fs[y]

    gqkv[...] = acc[...].astype(BF16)
    for k in range(1, NZ):
        arrived(tf.at[at_z(-k)], tz_s.at[k - 1], tz_r.at[k - 1])
    acc[:, 0:WIDTH] = sob[...].astype(F32)
    for i in range(NY):
        acc[:, 256 * i: 256 * i + 384] += window_of(tf, i)
    bo[...] = acc[:, 0:WIDTH].astype(BF16)

    for k in range(1, NY):
        arrived(fy.at[at_y(-k)], py_s.at[k - 1], py_r.at[k - 1])
    n = NX * NC
    for k in range(1, n):
        to = lax.rem(dp + k, n)
        send(fy, fd.at[dp], pd_s.at[k - 1], pd_r.at[k - 1], to, s)
    fd[dp] = fy[...]
    for k in range(1, n):
        arrived(fd.at[lax.rem(dp + n - k, n)], pd_s.at[k - 1], pd_r.at[k - 1])
    gwf[...] = jnp.zeros_like(gwf)
    lane = lax.broadcasted_iota(jnp.int32, (48, 384), 1)
    for g in range(NY):
        for i in range(3):
            tiles = [2 * i + t for t in range(3)]
            window = jnp.concatenate(
                [fd[2 * (t % 4) + t // 4, g].astype(F32) for t in tiles], axis=1
            )
            if i > 0:
                window = pltpu.roll(window, 384 - 32 * i, 1)
            window = jnp.where(lane < 288, window, 0.0)
            if g > 0:
                window = pltpu.roll(window, 32 * g, 1)
            at = WIDTH * i + 256 * g
            gwf[:, at: at + 384] += window
    picked = jnp.zeros((48, 432), F32)
    for d in range(n):
        picked = jnp.where(dp == d, gwf[:, 432 * d: 432 * d + 432], picked)
    gw[...] = picked[0:36].astype(BF16)

    for copy in sent:
        copy.wait_send()


def window_of(ref, i):
    return ref[:, i].reshape(128, 384).astype(F32)


def local(spatial_qkv, lengths, w_qkv, cotangent):
    frames, patches = spatial_qkv.shape[1], spatial_qkv.shape[2]
    vmem = pl.BlockSpec(memory_space=pltpu.VMEM)
    dma = pltpu.SemaphoreType.DMA

    def bf(*shape):
        return pltpu.VMEM(shape, BF16)

    def fl(*shape):
        return pltpu.VMEM(shape, F32)

    out = pl.pallas_call(
        kernel,
        out_shape=(
            jax.ShapeDtypeStruct((patches, WIDTH), BF16),
            jax.ShapeDtypeStruct((patches, 3 * WIDTH), BF16),
            jax.ShapeDtypeStruct((36, 432), BF16),
        ),
        in_specs=[pl.BlockSpec(memory_space=pltpu.SMEM), vmem, vmem, vmem],
        out_specs=(vmem, vmem, vmem),
        scratch_shapes=[
            fl(128, 3 * WIDTH),
            fl(16, 128, 128),
            bf(128, WIDTH),
            bf(4, 2, 48, 512),
            bf(4, 48, 512),
            fl(160, 512),
            bf(2, WIDTH, 512),
            bf(8, 4, 16, WIDTH),
            bf(4, 128, 384),
            bf(8, 4, 16, 384),
            fl(3, 512, 128),
            fl(7, 512, 128),
            fl(3, 512, 128),
            bf(8, 4, 16, 384),
            bf(4, 8, 16, 384),
            bf(8, 4, 16, 384),
            fl(7, 512, 128),
            bf(8, 4, 16, 1024),
            bf(4, 8, 16, WIDTH),
            bf(3, 8, 16, WIDTH),
            bf(8, 16, WIDTH),
            bf(8, 16, WIDTH),
            bf(2, WIDTH, 512),
            bf(WIDTH, 512),
            bf(WIDTH, 512),
            bf(3, WIDTH, 128),
            bf(8, 144, 128),
            bf(8, 144, 128),
            fl(160, 128),
            bf(4, 48, 128),
            bf(4, 48, 128),
            bf(8, 4, 48, 128),
            fl(48, 3 * WIDTH),
            dma((3,)), dma((3,)), dma((4,)), dma((4,)), dma((3,)), dma((3,)), dma((8,)), dma((8,)),
            dma((3,)), dma((3,)), dma((7,)), dma((7,)),
            dma((7,)), dma((7,)), dma((3,)), dma((3,)),
            dma((3,)), dma((3,)), dma((7,)), dma((7,)),
            dma((3,)), dma((3,)), dma((7,)), dma((7,)),
            dma, dma, dma((3,)), dma((3,)), dma((7,)), dma((7,)),
            dma((3,)), dma((3,)), dma((7,)), dma((7,)),
        ],
        compiler_params=pltpu.CompilerParams(
            collective_id=0, has_side_effects=True, vmem_limit_bytes=50 * 1024 * 1024
        ),
    )(
        lengths, spatial_qkv.reshape(patches, 3 * WIDTH), w_qkv,
        cotangent.reshape(patches, WIDTH),
    )
    return (
        out[0].reshape(1, frames, patches, WIDTH),
        out[1].reshape(1, frames, patches, 3 * WIDTH),
        out[2],
    )


def solution(mesh):
    in_specs = (P("dp", "seq", None, None), P("dp"), P("seq", None), P("dp", "seq", None, None))
    out_specs = (P("dp", "seq", None, None), P("dp", "seq", None, None), P("seq", "dp"))
    return jax.shard_map(local, mesh=mesh, in_specs=in_specs, out_specs=out_specs, check_vma=False)
```

```python
import jax
import jax.numpy as jnp
from jax import lax
from jax.experimental import pallas as pl
from jax.experimental.pallas import tpu as pltpu
from jax.sharding import PartitionSpec as P

HEADS = 16
WIDTH = 1152
HEAD = 72
NY, NZ, NX, NC = 4, 8, 4, 2
MESH = pl.DeviceIdType.MESH
F32, BF16 = jnp.float32, jnp.bfloat16
SCALE = HEAD ** (-0.5)


def dot(a, b):
    return lax.dot_general(a, b, (((1,), (0,)), ((), ())), preferred_element_type=F32)


def dot_nt(a, b):
    return lax.dot_general(a, b, (((1,), (1,)), ((), ())), preferred_element_type=F32)


def dot_tn(a, b):
    return lax.dot_general(a, b, (((0,), (0,)), ((), ())), preferred_element_type=F32)


def half(window, j):
    return window[:, 0:256] if j < 2 else window[:, 128:384]


def head_masks(off):
    lane = lax.broadcasted_iota(jnp.int32, (128, 256), 1)
    masks = []
    for j in range(4):
        low = off + HEAD * j - (128 if j >= 2 else 0)
        masks.append(jnp.where((lane >= low) & (lane < low + HEAD), 1.0, 0.0).astype(BF16))
    return masks


def join(parts):
    left, right = parts[0] + parts[1], parts[2] + parts[3]
    return jnp.concatenate(
        [left[:, 0:128], left[:, 128:256] + right[:, 0:128], right[:, 128:256]], axis=1
    )


def forward4(q, k, v, masks, live):
    probs, outs = [], []
    for j in range(4):
        scores = dot_nt(half(q, j) * masks[j], half(k, j)) * SCALE
        if live is not None:
            scores = jnp.where(live, scores, -1e30)
        expo = jnp.exp(scores - jnp.max(scores, axis=-1, keepdims=True))
        prob = expo * (1.0 / jnp.sum(expo, axis=-1, keepdims=True))
        probs.append(prob)
        outs.append(dot(prob.astype(BF16), half(v, j) * masks[j]))
    return join(outs), probs


def backward4(g, q, k, v, probs, masks):
    dqs, dks, dvs = [], [], []
    for j in range(4):
        prob = probs[j]
        gh = half(g, j) * masks[j]
        dvs.append(dot_tn(prob.astype(BF16), gh))
        gp = dot_nt(gh, half(v, j))
        gs = prob * (gp - jnp.sum(gp * prob, axis=-1, keepdims=True))
        low = (gs * SCALE).astype(BF16)
        dqs.append(dot(low, half(k, j) * masks[j]))
        dks.append(dot_tn(low, half(q, j) * masks[j]))
    return join(dqs), join(dks), join(dvs)


def remote(src, dst, ssem, rsem, dp, s):
    return pltpu.make_async_remote_copy(
        src_ref=src, dst_ref=dst, send_sem=ssem, recv_sem=rsem,
        device_id=(dp, s), device_id_type=MESH,
    )


def m16(value):
    return pl.multiple_of(value, 16)


Z_ORDER = (1, 7, 2, 6, 3, 5, 4)
BLOCK = 144
CHUNK = 384


def placed(group, tile):
    found = set()
    for part in range(3):
        low = max(128 * tile, 288 * part)
        high = min(128 * tile + 128, 288 * part + 288)
        if low < high:
            shift = WIDTH * part + 288 * group - 288 * part
            found |= set(range((low + shift) // 432, (high - 1 + shift) // 432 + 1))
    return sorted(found)


def tile_owner(tile):
    return 2 * (tile % 4) + tile // 4


def kernel(
    len_ref, qkv_h, w, cot_h, bo, gqkv, gw,
    qkv, cot, acc, prs, prt, blk, sob, wp, wr, wm, wf, so, cy, cz, c32, pj, to32, tob, ty, tf,
    gp32, gpb, gs, gr, gz, gf, grad, pw, crv, kr, xr, zr, zb, fr, fs, fy, fd, gwf,
    in_s, wy_s, wy_r, wz_s, wz_r, wx_s, wx_r, wd_s, wd_r, cy_s, cy_r, cz_s, cz_r,
    sz_s, sz_r, sy_s, sy_r, ty_s, ty_r, tz_s, tz_r, gy_s, gy_r, gz_s, gz_r,
    pc_s, pc_r, px_s, px_r, pz_s, pz_r, py_s, py_r, pd_s, pd_r,
):
    dp, s = lax.axis_index("dp"), lax.axis_index("seq")
    y, z = lax.rem(s, NY), lax.div(s, NY)
    c, x = lax.rem(dp, NC), lax.div(dp, NC)
    sib = x * NC + (1 - c)
    mine = 4 * c + x
    sent = []

    def at_y(k):
        return lax.rem(y + k + NY, NY)

    def at_z(k):
        return lax.rem(z + k + NZ, NZ)

    def at_x(k):
        return lax.rem(x + k + NX, NX)

    def send(src, dst, ssem, rsem, dp_to, s_to):
        copy = remote(src, dst, ssem, rsem, dp_to, s_to)
        copy.start()
        sent.append(copy)

    def arrived(dst, ssem, rsem):
        remote(dst, dst, ssem, rsem, dp, s).wait_recv()

    barrier = pltpu.get_barrier_semaphore()
    for k in range(1, NY):
        pl.semaphore_signal(barrier, inc=1, device_id=(dp, z * NY + at_y(k)), device_id_type=MESH)
    for k in range(1, NZ):
        pl.semaphore_signal(barrier, inc=1, device_id=(dp, at_z(k) * NY + y), device_id_type=MESH)
    for k in range(1, NX * NC):
        pl.semaphore_signal(
            barrier, inc=1, device_id=(lax.rem(dp + k, NX * NC), s), device_id_type=MESH
        )
    qkv_in = pltpu.make_async_copy(qkv_h, qkv, in_s.at[0])
    cot_in = pltpu.make_async_copy(cot_h, cot, in_s.at[1])
    qkv_in.start()
    cot_in.start()

    wrow = w[...].astype(F32)
    for g in range(NY):
        piece = jnp.concatenate(
            [wrow[:, 288 * g + WIDTH * i: 288 * g + WIDTH * i + 288] for i in range(3)]
            + [jnp.zeros((36, 160), F32)], axis=1
        )
        piece = jnp.concatenate([piece, jnp.zeros((12, 1024), F32)], axis=0).astype(BF16)
        for t in range(8):
            wp[g, t] = piece[:, 128 * t: 128 * t + 128]
    wr[y] = wp[y, mine]
    acc[...] = jnp.zeros_like(acc)
    fd[...] = jnp.zeros_like(fd)

    def spatial_forward(group):
        at = pl.multiple_of(256 * group, 128)
        q, k, v = (qkv[:, pl.ds(at + WIDTH * i, 384)] for i in range(3))
        out, probs = forward4(q, k, v, head_masks(32 * group), None)
        acc[:, pl.ds(at, 384)] += out
        for j in range(4):
            prs[4 * group + j] = probs[j]

    qkv_in.wait()
    cot_in.wait()
    spatial_forward(0)
    cy[y] = cot[:, pl.ds(pl.multiple_of(256 * y, 128), 384)]

    pl.semaphore_wait(barrier, NY + NZ + NX * NC - 3)
    for k in range(1, NY):
        to = at_y(k)
        send(wp.at[to, mine], wr.at[y], wy_s.at[k - 1], wy_r.at[k - 1], dp, z * NY + to)
    for k in range(1, NY):
        to = at_y(k)
        send(
            cot.at[:, pl.ds(pl.multiple_of(256 * to, 128), 384)], cy.at[y],
            cy_s.at[k - 1], cy_r.at[k - 1], dp, z * NY + to,
        )
    spatial_forward(1)
    spatial_forward(2)
    spatial_forward(3)
    sob[...] = acc[:, 0:WIDTH].astype(BF16)

    for k in range(1, NY):
        arrived(wr.at[at_y(-k)], wy_s.at[k - 1], wy_r.at[k - 1])
    for i in range(NY):
        wm[36 * i: 36 * i + 48, :] = wr[i].astype(F32)
    wf[mine, pl.ds(m16(BLOCK * z), BLOCK)] = wm[0:BLOCK, :].astype(BF16)

    def rows(k):
        return pl.ds(m16(BLOCK * at_z(k)), BLOCK)

    def weight_x(order, k):
        for i in range(1, NX):
            block = wf.at[mine, rows(k)]
            send(block, block, wx_s.at[order, i - 1], wx_r.at[order, i - 1], at_x(i) * NC + c, s)

    def spread_y(order, k):
        for i in range(1, NY):
            block = so.at[at_z(k), y]
            send(block, block, sy_s.at[order, i - 1], sy_r.at[order, i - 1], dp, z * NY + at_y(i))

    for k in Z_ORDER:
        block = wf.at[mine, rows(0)]
        send(block, block, wz_s.at[k - 1], wz_r.at[k - 1], dp, at_z(k) * NY + y)
    weight_x(0, 0)
    for k in Z_ORDER:
        to = at_z(k)
        send(
            sob.at[pl.ds(m16(16 * to), 16)], so.at[z, y],
            sz_s.at[k - 1], sz_r.at[k - 1], dp, to * NY + y,
        )
    so[z, y] = sob[pl.ds(m16(16 * z), 16), :]
    spread_y(0, 0)
    for order, k in enumerate(Z_ORDER):
        arrived(wf.at[mine, rows(-k)], wz_s.at[k - 1], wz_r.at[k - 1])
        weight_x(order + 1, -k)
        arrived(so.at[at_z(-k), y], sz_s.at[k - 1], sz_r.at[k - 1])
        spread_y(order + 1, -k)

    for k in range(1, NY):
        arrived(cy.at[at_y(-k)], cy_s.at[k - 1], cy_r.at[k - 1])
    for k in Z_ORDER:
        to = at_z(k)
        send(
            cy.at[:, pl.ds(m16(16 * to), 16)], cz.at[z],
            cz_s.at[k - 1], cz_r.at[k - 1], dp, to * NY + y,
        )
    cz[z] = cy[:, pl.ds(m16(16 * z), 16), :]

    for order, k in enumerate((0,) + Z_ORDER):
        for i in range(1, NX):
            arrived(
                wf.at[4 * c + at_x(-i), rows(-k)], wx_s.at[order, i - 1], wx_r.at[order, i - 1]
            )
        block = wf.at[pl.ds(4 * c, 4), rows(-k)]
        send(block, block, wd_s.at[order], wd_r.at[order], sib, s)
    for order, k in enumerate((0,) + Z_ORDER):
        for i in range(1, NY):
            arrived(so.at[at_z(-k), at_y(-i)], sy_s.at[order, i - 1], sy_r.at[order, i - 1])
    for order, k in enumerate((0,) + Z_ORDER):
        arrived(wf.at[pl.ds(4 - 4 * c, 4), rows(-k)], wd_s.at[order], wd_r.at[order])

    every = so[...].reshape(512, WIDTH)
    for t in range(4):
        if t < 3:
            pair = dot(every, jnp.concatenate([wf[2 * t], wf[2 * t + 1]], axis=1))
            pj[2 * t], pj[2 * t + 1] = pair[:, 0:128], pair[:, 128:256]
        else:
            pj[6] = dot(every, wf[6])

    length = len_ref[0]
    row = lax.broadcasted_iota(jnp.int32, (128, 128), 0)
    col = lax.broadcasted_iota(jnp.int32, (128, 128), 1)
    live = ((row >> 5) == (col >> 5)) & ((col & 31) < length)
    masks = head_masks(0)

    def rows_of(ref, first, b):
        return jnp.concatenate(
            [
                jnp.concatenate(
                    [ref[t, pl.ds(4 * b + i, 32, stride=16), :] for i in range(4)], axis=0
                )
                for t in range(first, first + 3)
            ],
            axis=1,
        )

    def temporal_forward(b, carry):
        q = rows_of(pj, 0, b).astype(BF16)
        k = pltpu.roll(rows_of(pj, 2, b), 384 - 32, 1).astype(BF16)
        v = pltpu.roll(rows_of(pj, 4, b), 384 - 64, 1).astype(BF16)
        blk[b, 0], blk[b, 1], blk[b, 2] = q, k, v
        out, probs = forward4(q, k, v, masks, live)
        for j in range(4):
            prt[b, j] = probs[j]
        for i in range(4):
            for t in range(3):
                to32[t, pl.ds(4 * b + i, 32, stride=16), :] = out[
                    32 * i: 32 * i + 32, 128 * t: 128 * t + 128
                ]
        return carry

    lax.fori_loop(0, 4, temporal_forward, 0)

    t_out = jnp.concatenate([to32[t] for t in range(3)], axis=1)
    turned = t_out
    for k in range(1, NY):
        turned = jnp.where(y == k, pltpu.roll(t_out, 32 * k, 1), turned)
    tob[...] = turned.astype(BF16).reshape(NZ, NY, 16, 384)
    for k in range(1, NY):
        to = at_y(k)
        send(tob.at[:, to], ty.at[y], ty_s.at[k - 1], ty_r.at[k - 1], dp, z * NY + to)
    ty[y] = tob[:, y]

    for k in Z_ORDER:
        arrived(cz.at[at_z(-k)], cz_s.at[k - 1], cz_r.at[k - 1])
    g_in = cz[...].reshape(512, 384).astype(F32)
    turned = g_in
    for k in range(1, NY):
        turned = jnp.where(y == k, pltpu.roll(g_in, 384 - 32 * k, 1), turned)
    for t in range(3):
        c32[t] = turned[:, 128 * t: 128 * t + 128]

    def temporal_backward(b, carry):
        q, k, v = blk[b, 0], blk[b, 1], blk[b, 2]
        g = rows_of(c32, 0, b).astype(BF16)
        dq, dk, dv = backward4(g, q, k, v, [prt[b, j] for j in range(4)], masks)
        dk, dv = pltpu.roll(dk, 32, 1), pltpu.roll(dv, 64, 1)
        packed = jnp.concatenate(
            [dq[:, 0:256], dq[:, 256:384] + dk[:, 0:128], dk[:, 128:256],
             dk[:, 256:384] + dv[:, 0:128], dv[:, 128:384]], axis=1
        )
        for i in range(4):
            for t in range(7):
                gp32[t, pl.ds(4 * b + i, 32, stride=16), :] = packed[
                    32 * i: 32 * i + 32, 128 * t: 128 * t + 128
                ]
        return carry

    lax.fori_loop(0, 4, temporal_backward, 0)

    for t in range(7):
        gpb[:, 128 * t: 128 * t + 128] = gp32[t].astype(BF16)
    gpb[:, 896:1024] = jnp.zeros((512, 128), BF16)

    def weight_chunk(i):
        at = CHUNK * i
        part = dot_tn(so[:, :, :, at: at + CHUNK].reshape(512, CHUNK), gpb[...]).astype(BF16)
        for t in range(8):
            pw[t, at: at + CHUNK] = part[:, 128 * t: 128 * t + 128]
        send(
            pw.at[pl.ds(4 - 4 * c, 4), at: at + CHUNK], crv.at[:, at: at + CHUNK],
            pc_s.at[i], pc_r.at[i], sib, s,
        )

    def back_chunk(i):
        at = CHUNK * i
        part = jnp.zeros((512, CHUNK), F32)
        for t in range(4):
            if t < 3:
                weight = jnp.concatenate(
                    [wf[2 * t, at: at + CHUNK], wf[2 * t + 1, at: at + CHUNK]], axis=1
                )
                part = part + dot_nt(gpb[:, 256 * t: 256 * t + 256], weight)
            else:
                part = part + dot_nt(gpb[:, 768:896], wf[6, at: at + CHUNK])
        gs[i] = part.astype(BF16).reshape(NZ, NY, 16, CHUNK)
        for k in range(1, NY):
            to = at_y(k)
            send(
                gs.at[i, :, to], gr.at[i, k - 1],
                gy_s.at[i, k - 1], gy_r.at[i, k - 1], dp, z * NY + to,
            )

    def weight_sum(i):
        at = CHUNK * i
        arrived(crv.at[:, at: at + CHUNK], pc_s.at[i], pc_r.at[i])
        kr[:, at: at + CHUNK] = (
            pw[pl.ds(4 * c, 4), at: at + CHUNK].astype(F32) + crv[:, at: at + CHUNK].astype(F32)
        ).astype(BF16)
        for k in range(1, NX):
            to = at_x(k)
            send(
                kr.at[to, at: at + CHUNK], xr.at[k - 1, at: at + CHUNK],
                px_s.at[i, k - 1], px_r.at[i, k - 1], to * NC + c, s,
            )

    def weight_z(i, blocks):
        at = CHUNK * i
        for k in range(1, NX):
            arrived(xr.at[k - 1, at: at + CHUNK], px_s.at[i, k - 1], px_r.at[i, k - 1])
        total = kr[x, at: at + CHUNK].astype(F32)
        for k in range(1, NX):
            total = total + xr[k - 1, at: at + CHUNK].astype(F32)
        zr[at: at + CHUNK] = total.astype(BF16)
        for b in blocks:
            @pl.when(z != b)
            def _():
                remote(
                    zr.at[BLOCK * b: BLOCK * b + BLOCK], zb.at[z],
                    pz_s.at[b], pz_r.at[z], dp, b * NY + y,
                ).start()

    def back_sum(i):
        for k in range(1, NY):
            arrived(gr.at[i, k - 1], gy_s.at[i, k - 1], gy_r.at[i, k - 1])
        total = gs[i, :, y].astype(F32)
        for k in range(1, NY):
            total = total + gr[i, k - 1].astype(F32)
        gz[i] = total.astype(BF16)
        for k in Z_ORDER:
            to = at_z(k)
            send(
                gz.at[i, to], gf.at[i, z], gz_s.at[i, k - 1], gz_r.at[i, k - 1], dp, to * NY + y
            )
        gf[i, z] = gz[i, z]

    def back_done(i):
        at = CHUNK * i
        for k in Z_ORDER:
            arrived(gf.at[i, at_z(-k)], gz_s.at[i, k - 1], gz_r.at[i, k - 1])
        grad[:, at: at + CHUNK] = (
            cot[:, at: at + CHUNK].astype(F32) + gf[i].reshape(128, CHUNK).astype(F32)
        ).astype(BF16)

    def spatial_backward(group):
        at = 256 * group
        q, k, v = (qkv[:, at + WIDTH * i: at + WIDTH * i + 384] for i in range(3))
        probs = [prs[4 * group + j] for j in range(4)]
        grads = backward4(grad[:, at: at + 384], q, k, v, probs, head_masks(32 * group))
        for i in range(3):
            acc[:, at + WIDTH * i: at + WIDTH * i + 384] += grads[i]

    weight_chunk(0)
    back_chunk(0)
    weight_chunk(1)
    weight_sum(0)
    weight_chunk(2)
    weight_sum(1)
    back_chunk(1)
    back_chunk(2)
    weight_sum(2)

    for k in range(1, NY):
        arrived(ty.at[at_y(-k)], ty_s.at[k - 1], ty_r.at[k - 1])
    for k in Z_ORDER:
        to = at_z(k)
        send(ty.at[:, to], tf.at[z], tz_s.at[k - 1], tz_r.at[k - 1], dp, to * NY + y)
    tf[z] = ty[:, z]
    acc[...] = jnp.zeros_like(acc)

    back_sum(0)
    weight_z(0, (0, 1))
    back_sum(1)
    weight_z(1, (2, 3, 4))
    back_sum(2)
    back_done(0)
    spatial_backward(0)
    weight_z(2, (5, 6, 7))
    back_done(1)
    spatial_backward(1)
    back_done(2)
    spatial_backward(2)
    spatial_backward(3)

    zb[z] = zr[pl.ds(m16(BLOCK * z), BLOCK)]
    for b in range(NZ):
        @pl.when(z != b)
        def _():
            arrived(zb.at[b], pz_s.at[b], pz_r.at[b])
    total = zb[0].astype(F32)
    for i in range(1, NZ):
        total = total + zb[i].astype(F32)
    fr[0:BLOCK, :] = total
    fr[BLOCK:160, :] = jnp.zeros((16, 128), F32)
    for i in range(NY):
        fs[i] = fr[36 * i: 36 * i + 48, :].astype(BF16)
    for k in range(1, NY):
        to = at_y(k)
        send(fs.at[to], fy.at[y], py_s.at[k - 1], py_r.at[k - 1], dp, z * NY + to)
    fy[y] = fs[y]

    gqkv[...] = acc[...].astype(BF16)
    for k in Z_ORDER:
        arrived(tf.at[at_z(-k)], tz_s.at[k - 1], tz_r.at[k - 1])
    acc[:, 0:WIDTH] = sob[...].astype(F32)
    for i in range(NY):
        acc[:, 256 * i: 256 * i + 384] += tf[:, i].reshape(128, 384).astype(F32)
    bo[...] = acc[:, 0:WIDTH].astype(BF16)

    for k in range(1, NY):
        arrived(fy.at[at_y(-k)], py_s.at[k - 1], py_r.at[k - 1])

    def moves(tile):
        return [
            (g, d) for g in range(NY) for d in placed(g, tile) if d != tile_owner(tile)
        ]

    def move(tile, g, d):
        return remote(fy.at[g], fd.at[tile, g], pd_s.at[g, d], pd_r.at[tile, g], d, s)

    for tile in range(7):
        @pl.when(dp == tile_owner(tile))
        def _():
            for g, d in moves(tile):
                move(tile, g, d).start()
    fd[mine] = fy[...]
    for d in range(NX * NC):
        @pl.when(dp == d)
        def _():
            for tile in range(7):
                for g, to in moves(tile):
                    if to == d:
                        arrived(fd.at[tile, g], pd_s.at[g, d], pd_r.at[tile, g])
    gwf[...] = jnp.zeros_like(gwf)
    lane = lax.broadcasted_iota(jnp.int32, (48, 384), 1)
    for g in range(NY):
        for i in range(3):
            window = jnp.concatenate(
                [fd[2 * i + t, g].astype(F32) for t in range(3)], axis=1
            )
            if i > 0:
                window = pltpu.roll(window, 384 - 32 * i, 1)
            window = jnp.where(lane < 288, window, 0.0)
            if g > 0:
                window = pltpu.roll(window, 32 * g, 1)
            at = WIDTH * i + 256 * g
            gwf[:, at: at + 384] += window
    picked = jnp.zeros((48, 432), F32)
    for d in range(NX * NC):
        picked = jnp.where(dp == d, gwf[:, 432 * d: 432 * d + 432], picked)
    gw[...] = picked[0:36].astype(BF16)

    for copy in sent:
        copy.wait_send()
    for b in range(NZ):
        @pl.when(z != b)
        def _():
            remote(
                zr.at[BLOCK * b: BLOCK * b + BLOCK], zb.at[z], pz_s.at[b], pz_r.at[z], dp, s
            ).wait_send()
    for tile in range(7):
        @pl.when(dp == tile_owner(tile))
        def _():
            for g, d in moves(tile):
                move(tile, g, d).wait_send()


def local(spatial_qkv, lengths, w_qkv, cotangent):
    frames, patches = spatial_qkv.shape[1], spatial_qkv.shape[2]
    vmem = pl.BlockSpec(memory_space=pltpu.VMEM)
    anywhere = pl.BlockSpec(memory_space=pltpu.HBM)
    dma = pltpu.SemaphoreType.DMA

    def bf(*shape):
        return pltpu.VMEM(shape, BF16)

    def fl(*shape):
        return pltpu.VMEM(shape, F32)

    out = pl.pallas_call(
        kernel,
        out_shape=(
            jax.ShapeDtypeStruct((patches, WIDTH), BF16),
            jax.ShapeDtypeStruct((patches, 3 * WIDTH), BF16),
            jax.ShapeDtypeStruct((36, 432), BF16),
        ),
        in_specs=[pl.BlockSpec(memory_space=pltpu.SMEM), anywhere, vmem, anywhere],
        out_specs=(vmem, vmem, vmem),
        scratch_shapes=[
            bf(128, 3 * WIDTH),
            bf(128, WIDTH),
            fl(128, 3 * WIDTH),
            fl(16, 128, 128),
            fl(4, 4, 128, 128),
            bf(4, 3, 128, 384),
            bf(128, WIDTH),
            bf(4, 8, 48, 128),
            bf(4, 48, 128),
            fl(160, 128),
            bf(8, WIDTH, 128),
            bf(8, 4, 16, WIDTH),
            bf(4, 128, 384),
            bf(8, 4, 16, 384),
            fl(3, 512, 128),
            fl(7, 512, 128),
            fl(3, 512, 128),
            bf(8, 4, 16, 384),
            bf(4, 8, 16, 384),
            bf(8, 4, 16, 384),
            fl(7, 512, 128),
            bf(512, 1024),
            bf(3, 8, 4, 16, CHUNK),
            bf(3, 3, 8, 16, CHUNK),
            bf(3, 8, 16, CHUNK),
            bf(3, 8, 16, CHUNK),
            bf(128, WIDTH),
            bf(8, WIDTH, 128),
            bf(4, WIDTH, 128),
            bf(4, WIDTH, 128),
            bf(3, WIDTH, 128),
            bf(WIDTH, 128),
            bf(8, BLOCK, 128),
            fl(160, 128),
            bf(4, 48, 128),
            bf(4, 48, 128),
            bf(8, 4, 48, 128),
            fl(48, 3 * WIDTH),
            dma((2,)), dma((3,)), dma((3,)), dma((7,)), dma((7,)),
            dma((8, 3)), dma((8, 3)), dma((8,)), dma((8,)),
            dma((3,)), dma((3,)), dma((7,)), dma((7,)),
            dma((7,)), dma((7,)), dma((8, 3)), dma((8, 3)),
            dma((3,)), dma((3,)), dma((7,)), dma((7,)),
            dma((3, 3)), dma((3, 3)), dma((3, 7)), dma((3, 7)),
            dma((3,)), dma((3,)), dma((3, 3)), dma((3, 3)), dma((8,)), dma((8,)),
            dma((3,)), dma((3,)), dma((4, 8)), dma((8, 4)),
        ],
        compiler_params=pltpu.CompilerParams(
            collective_id=0, has_side_effects=True, vmem_limit_bytes=50 * 1024 * 1024
        ),
    )(
        lengths, spatial_qkv.reshape(patches, 3 * WIDTH), w_qkv,
        cotangent.reshape(patches, WIDTH),
    )
    return (
        out[0].reshape(1, frames, patches, WIDTH),
        out[1].reshape(1, frames, patches, 3 * WIDTH),
        out[2],
    )


def solution(mesh):
    in_specs = (P("dp", "seq", None, None), P("dp"), P("seq", None), P("dp", "seq", None, None))
    out_specs = (P("dp", "seq", None, None), P("dp", "seq", None, None), P("seq", "dp"))
    return jax.shard_map(local, mesh=mesh, in_specs=in_specs, out_specs=out_specs, check_vma=False)
```

```python
import jax
import jax.numpy as jnp
from jax import lax
from jax.experimental import pallas as pl
from jax.experimental.pallas import tpu as pltpu
from jax.sharding import PartitionSpec as P

HEADS = 16
WIDTH = 1152
HEAD = 72
NY, NZ, NX, NC = 4, 8, 4, 2
MESH = pl.DeviceIdType.MESH
F32, BF16 = jnp.float32, jnp.bfloat16
SCALE = HEAD ** (-0.5)


def dot(a, b):
    return lax.dot_general(a, b, (((1,), (0,)), ((), ())), preferred_element_type=F32)


def dot_nt(a, b):
    return lax.dot_general(a, b, (((1,), (1,)), ((), ())), preferred_element_type=F32)


def dot_tn(a, b):
    return lax.dot_general(a, b, (((0,), (0,)), ((), ())), preferred_element_type=F32)


def half(window, pair):
    return window[:, 0:256] if pair == 0 else window[:, 128:384]


def head_masks(off):
    lane = lax.broadcasted_iota(jnp.int32, (128, 256), 1)
    masks = []
    for j in range(4):
        low = off + HEAD * j - (128 if j >= 2 else 0)
        masks.append(jnp.where((lane >= low) & (lane < low + HEAD), 1.0, 0.0).astype(BF16))
    return masks


def two(window, pair, masks):
    own = half(window, pair)
    return jnp.concatenate([own * masks[2 * pair], own * masks[2 * pair + 1]], axis=0)


def stack(array):
    return jnp.concatenate([array[:, 0:128], array[:, 128:256]], axis=0)


def join(parts):
    left, right = parts
    return jnp.concatenate(
        [left[:, 0:128], left[:, 128:256] + right[:, 0:128], right[:, 128:256]], axis=1
    )


def forward4(q, k, v, masks, live):
    probs, outs = [], []
    for pair in range(2):
        scores = dot_nt(half(k, pair), two(q, pair, masks)) * SCALE
        if live is not None:
            scores = jnp.where(live, scores, -1e30)
        expo = jnp.exp(scores - jnp.max(scores, axis=0, keepdims=True))
        prob = expo * (1.0 / jnp.sum(expo, axis=0, keepdims=True))
        probs.append(prob)
        outs.append(dot_tn(stack(prob.astype(BF16)), two(v, pair, masks)))
    return join(outs), probs


def backward4(g, q, k, v, probs, masks, values=True):
    dqs, dks, dvs = [], [], []
    for pair in range(2):
        prob = probs[pair]
        g_two = two(g, pair, masks)
        if values:
            dvs.append(dot(prob.astype(BF16), g_two))
        gp = dot_nt(half(v, pair), g_two)
        gs = prob * (gp - jnp.sum(gp * prob, axis=0, keepdims=True))
        low = (gs * SCALE).astype(BF16)
        dqs.append(dot_tn(stack(low), two(k, pair, masks)))
        dks.append(dot(low, two(q, pair, masks)))
    return (join(dqs), join(dks)) + ((join(dvs),) if values else ())


def remote(src, dst, ssem, rsem, dp, s):
    return pltpu.make_async_remote_copy(
        src_ref=src, dst_ref=dst, send_sem=ssem, recv_sem=rsem,
        device_id=(dp, s), device_id_type=MESH,
    )


def m16(value):
    return pl.multiple_of(value, 16)


Z_ORDER = (1, 7, 2, 6, 3, 5, 4)
BLOCK = 144
CHUNK = 384


PART_AT = (2 * WIDTH, 0, WIDTH)
OWNER = (0, 6, 1, 2, 3, 4, 5, 7)


def placed(group, tile):
    found = set()
    for part in range(3):
        low = max(128 * tile, 288 * part)
        high = min(128 * tile + 128, 288 * part + 288)
        if low < high:
            shift = PART_AT[part] + 288 * group - 288 * part
            found |= set(range((low + shift) // 432, (high - 1 + shift) // 432 + 1))
    return sorted(found)


def tile_owner(tile):
    return 2 * (OWNER[tile] % 4) + OWNER[tile] // 4


def kernel(
    len_ref, qkv_h, w, cot_h, bo, gqkv, gw,
    qkv, cot, acc, prs, prt, blk, sob, wp, wr, wm, wf, so, cy, cz, c32, pj, to32, tob, ty, tw, tf,
    gp32, gpb, gs, gr, gz, gf, grad, pw, dv2, cre, kre, crv, kr, xr, zr, zb, fr, fs, fy, fd, gwf,
    in_s, wy_s, wy_r, wz_s, wz_r, wx_s, wx_r, wd_s, wd_r, cy_s, cy_r, cz_s, cz_r,
    sz_s, sz_r, sy_s, sy_r, ty_s, ty_r, tz_s, tz_r, gy_s, gy_r, gz_s, gz_r,
    pe_s, pe_r, pxe_s, pxe_r, pc_s, pc_r, px_s, px_r, pz_s, pz_r, py_s, py_r, pd_s, pd_r,
):
    dp, s = lax.axis_index("dp"), lax.axis_index("seq")
    y, z = lax.rem(s, NY), lax.div(s, NY)
    c, x = lax.rem(dp, NC), lax.div(dp, NC)
    sib = x * NC + (1 - c)
    mine = 4 * c + x
    sent = []

    def at_y(k):
        return lax.rem(y + k + NY, NY)

    def at_z(k):
        return lax.rem(z + k + NZ, NZ)

    def at_x(k):
        return lax.rem(x + k + NX, NX)

    def send(src, dst, ssem, rsem, dp_to, s_to):
        copy = remote(src, dst, ssem, rsem, dp_to, s_to)
        copy.start()
        sent.append(copy)

    def arrived(dst, ssem, rsem):
        remote(dst, dst, ssem, rsem, dp, s).wait_recv()

    barrier = pltpu.get_barrier_semaphore()
    for k in range(1, NY):
        pl.semaphore_signal(barrier, inc=1, device_id=(dp, z * NY + at_y(k)), device_id_type=MESH)
    for k in range(1, NZ):
        pl.semaphore_signal(barrier, inc=1, device_id=(dp, at_z(k) * NY + y), device_id_type=MESH)
    for k in range(1, NX * NC):
        pl.semaphore_signal(
            barrier, inc=1, device_id=(lax.rem(dp + k, NX * NC), s), device_id_type=MESH
        )
    qkv_in = pltpu.make_async_copy(qkv_h, qkv, in_s.at[0])
    cot_in = pltpu.make_async_copy(cot_h, cot, in_s.at[1])
    qkv_in.start()
    cot_in.start()

    wrow = w[...].astype(F32)
    for g in range(NY):
        piece = jnp.concatenate(
            [wrow[:, 288 * g + at: 288 * g + at + 288] for at in PART_AT]
            + [jnp.zeros((36, 160), F32)], axis=1
        )
        piece = jnp.concatenate([piece, jnp.zeros((12, 1024), F32)], axis=0).astype(BF16)
        for t in range(8):
            wp[g, OWNER[t]] = piece[:, 128 * t: 128 * t + 128]
    wr[y] = wp[y, mine]

    def spatial_forward(group):
        at = pl.multiple_of(256 * group, 128)
        q, k, v = (qkv[:, pl.ds(at + WIDTH * i, 384)] for i in range(3))
        out, probs = forward4(q, k, v, head_masks(32 * group), None)
        acc[:, pl.ds(at, 384)] += out
        for j in range(2):
            prs[2 * group + j] = probs[j]


    pl.semaphore_wait(barrier, NY + NZ + NX * NC - 3)
    for k in range(1, NY):
        to = at_y(k)
        send(wp.at[to, mine], wr.at[y], wy_s.at[k - 1], wy_r.at[k - 1], dp, z * NY + to)
    acc[...] = jnp.zeros_like(acc)
    fd[...] = jnp.zeros_like(fd)
    cot_in.wait()
    cy[y] = cot[:, pl.ds(pl.multiple_of(256 * y, 128), 384)]
    for k in range(1, NY):
        to = at_y(k)
        send(
            cot.at[:, pl.ds(pl.multiple_of(256 * to, 128), 384)], cy.at[y],
            cy_s.at[k - 1], cy_r.at[k - 1], dp, z * NY + to,
        )

    qkv_in.wait()
    for group in range(4):
        spatial_forward(group)
    sob[...] = acc[:, 0:WIDTH].astype(BF16)
    so[z, y] = sob[pl.ds(m16(16 * z), 16), :]

    for k in range(1, NY):
        arrived(wr.at[at_y(-k)], wy_s.at[k - 1], wy_r.at[k - 1])
    for i in range(NY):
        wm[36 * i: 36 * i + 48, :] = wr[i].astype(F32)
    wf[mine, pl.ds(m16(BLOCK * z), BLOCK)] = wm[0:BLOCK, :].astype(BF16)

    def rows(k):
        return pl.ds(m16(BLOCK * at_z(k)), BLOCK)

    def weight_x(order, k):
        for i in range(1, NX):
            block = wf.at[mine, rows(k)]
            send(block, block, wx_s.at[order, i - 1], wx_r.at[order, i - 1], at_x(i) * NC + c, s)

    def spread_y(order, k):
        for i in range(1, NY):
            block = so.at[at_z(k), y]
            send(block, block, sy_s.at[order, i - 1], sy_r.at[order, i - 1], dp, z * NY + at_y(i))

    def weight_on(k, step, way):
        block = wf.at[mine, rows(k)]
        send(block, block, wz_s.at[way - 1], wz_r.at[way - 1], dp, at_z(step) * NY + y)

    for k in (1, 7, 2, 6):
        weight_on(0, k, k)
    weight_x(0, 0)
    for k in Z_ORDER:
        to = at_z(k)
        send(
            sob.at[pl.ds(m16(16 * to), 16)], so.at[z, y],
            sz_s.at[k - 1], sz_r.at[k - 1], dp, to * NY + y,
        )
    spread_y(0, 0)
    for order, k in enumerate(Z_ORDER):
        arrived(wf.at[mine, rows(-k)], wz_s.at[k - 1], wz_r.at[k - 1])
        if k == 2:
            weight_on(-2, 1, 3)
            weight_on(-2, 2, 4)
        if k == 6:
            weight_on(2, -1, 5)
        weight_x(order + 1, -k)
        arrived(so.at[at_z(-k), y], sz_s.at[k - 1], sz_r.at[k - 1])
        spread_y(order + 1, -k)

    for k in range(1, NY):
        arrived(cy.at[at_y(-k)], cy_s.at[k - 1], cy_r.at[k - 1])
    for k in Z_ORDER:
        to = at_z(k)
        send(
            cy.at[:, pl.ds(m16(16 * to), 16)], cz.at[z],
            cz_s.at[k - 1], cz_r.at[k - 1], dp, to * NY + y,
        )
    cz[z] = cy[:, pl.ds(m16(16 * z), 16), :]

    for order, k in enumerate((0,) + Z_ORDER):
        for i in range(1, NX):
            arrived(
                wf.at[4 * c + at_x(-i), rows(-k)], wx_s.at[order, i - 1], wx_r.at[order, i - 1]
            )
        block = wf.at[pl.ds(4 * c, 4), rows(-k)]
        send(block, block, wd_s.at[order], wd_r.at[order], sib, s)
    for order, k in enumerate((0,) + Z_ORDER):
        for i in range(1, NY):
            arrived(so.at[at_z(-k), at_y(-i)], sy_s.at[order, i - 1], sy_r.at[order, i - 1])
    for order, k in enumerate((0,) + Z_ORDER):
        arrived(wf.at[pl.ds(4 - 4 * c, 4), rows(-k)], wd_s.at[order], wd_r.at[order])

    every = so[...].reshape(512, WIDTH)
    for t in range(4):
        if t < 3:
            pair = dot(
                every, jnp.concatenate([wf[OWNER[2 * t]], wf[OWNER[2 * t + 1]]], axis=1)
            )
            pj[2 * t], pj[2 * t + 1] = pair[:, 0:128], pair[:, 128:256]
        else:
            pj[6] = dot(every, wf[OWNER[6]])

    length = len_ref[0]
    key = lax.broadcasted_iota(jnp.int32, (128, 256), 0)
    query = lax.broadcasted_iota(jnp.int32, (128, 256), 1) & 127
    live = ((key >> 5) == (query >> 5)) & ((key & 31) < length)
    masks = head_masks(0)

    def rows_of(ref, first, b):
        return jnp.concatenate(
            [
                jnp.concatenate(
                    [ref[t, pl.ds(4 * b + i, 32, stride=16), :] for i in range(4)], axis=0
                )
                for t in range(first, first + 3)
            ],
            axis=1,
        )

    def temporal_forward(b, carry):
        v = rows_of(pj, 0, b).astype(BF16)
        q = pltpu.roll(rows_of(pj, 2, b), 384 - 32, 1).astype(BF16)
        k = pltpu.roll(rows_of(pj, 4, b), 384 - 64, 1).astype(BF16)
        blk[b, 0], blk[b, 1], blk[b, 2] = q, k, v
        out, probs = forward4(q, k, v, masks, live)
        for j in range(2):
            prt[b, j] = probs[j]
        for i in range(4):
            for t in range(3):
                to32[t, pl.ds(4 * b + i, 32, stride=16), :] = out[
                    32 * i: 32 * i + 32, 128 * t: 128 * t + 128
                ]
        return carry

    for b in range(0, 4):
        temporal_forward(b, 0)

    t_out = jnp.concatenate([to32[t] for t in range(3)], axis=1)
    turned = t_out
    for k in range(1, NY):
        turned = jnp.where(y == k, pltpu.roll(t_out, 32 * k, 1), turned)
    tob[...] = turned.astype(BF16).reshape(NZ, NY, 16, 384)
    for k in range(1, NY):
        to = at_y(k)
        send(tob.at[:, to], ty.at[y], ty_s.at[k - 1], ty_r.at[k - 1], dp, z * NY + to)
    ty[y] = tob[:, y]

    for k in Z_ORDER:
        arrived(cz.at[at_z(-k)], cz_s.at[k - 1], cz_r.at[k - 1])
    g_in = cz[...].reshape(512, 384).astype(F32)
    turned = g_in
    for k in range(1, NY):
        turned = jnp.where(y == k, pltpu.roll(g_in, 384 - 32 * k, 1), turned)
    for t in range(3):
        c32[t] = turned[:, 128 * t: 128 * t + 128]

    def scatter(ref, first, b, array):
        for i in range(4):
            for t in range(array.shape[1] // 128):
                ref[first + t, pl.ds(4 * b + i, 32, stride=16), :] = array[
                    32 * i: 32 * i + 32, 128 * t: 128 * t + 128
                ]

    def temporal_values(b, carry):
        g = rows_of(c32, 0, b).astype(BF16)
        blk[b, 3] = g
        dv = join([
            dot(prt[b, pair].astype(BF16), two(g, pair, masks)) for pair in range(2)
        ])
        scatter(gp32, 0, b, dv[:, 0:256])
        dv2[b] = dv[:, 256:384]
        return carry

    def temporal_backward(b, carry):
        q, k, v, g = blk[b, 0], blk[b, 1], blk[b, 2], blk[b, 3]
        dq, dk = backward4(g, q, k, v, [prt[b, j] for j in range(2)], masks, False)
        dq, dk = pltpu.roll(dq, 32, 1), pltpu.roll(dk, 64, 1)
        packed = jnp.concatenate(
            [dv2[b] + dq[:, 0:128], dq[:, 128:256], dq[:, 256:384] + dk[:, 0:128], dk[:, 128:384]],
            axis=1,
        )
        scatter(gp32, 2, b, packed)
        return carry

    def weight_part(at, low, high):
        part = dot_tn(
            so[:, :, :, at: at + CHUNK].reshape(512, CHUNK), gpb[:, 128 * low: 128 * high]
        ).astype(BF16)
        for t in range(low, high):
            pw[OWNER[t], at: at + CHUNK] = part[:, 128 * (t - low): 128 * (t - low) + 128]

    early, late = x == 2 * c, (x != 2 * c) & (mine != 7)

    def early_weight():
        for i in range(3):
            weight_part(CHUNK * i, 0, 2)
        send(pw.at[6 - 6 * c], cre, pe_s, pe_r, sib, s)

    def early_to():
        k = lax.rem(2 * c - x + NX, NX)
        slot = jnp.maximum(k - 1, 0)
        return remote(
            kre, xr.at[slot], pxe_s, pxe_r.at[slot], 2 * c * NC + c, s
        )

    def early_sum():
        arrived(cre, pe_s, pe_r)
        kre[...] = (pw[6 * c].astype(F32) + cre[...].astype(F32)).astype(BF16)

        @pl.when(x != 2 * c)
        def _():
            early_to().start()

    for b in range(0, 4):
        temporal_values(b, 0)
    for t in range(2):
        gpb[:, 128 * t: 128 * t + 128] = gp32[t].astype(BF16)
    early_weight()
    for b in range(0, 2):
        temporal_backward(b, 0)
    early_sum()
    for b in range(2, 4):
        temporal_backward(b, 0)
    for t in range(2, 7):
        gpb[:, 128 * t: 128 * t + 128] = gp32[t].astype(BF16)

    def weight_chunk(i):
        at = CHUNK * i
        weight_part(at, 2, 7)
        send(
            pw.at[pl.ds(4 - 3 * c, 3), at: at + CHUNK], crv.at[:, at: at + CHUNK],
            pc_s.at[i], pc_r.at[i], sib, s,
        )

    def back_chunk(i):
        at = CHUNK * i
        part = jnp.zeros((512, CHUNK), F32)
        for t in range(4):
            if t < 3:
                weight = jnp.concatenate(
                    [wf[OWNER[2 * t], at: at + CHUNK], wf[OWNER[2 * t + 1], at: at + CHUNK]],
                    axis=1,
                )
                part = part + dot_nt(gpb[:, 256 * t: 256 * t + 256], weight)
            else:
                part = part + dot_nt(gpb[:, 768:896], wf[OWNER[6], at: at + CHUNK])
        gs[i] = part.astype(BF16).reshape(NZ, NY, 16, CHUNK)
        for k in range(1, NY):
            to = at_y(k)
            send(
                gs.at[i, :, to], gr.at[i, k - 1],
                gy_s.at[i, k - 1], gy_r.at[i, k - 1], dp, z * NY + to,
            )

    def late_to(i, k):
        at = CHUNK * i
        to = at_x(k)
        wanted = (to != 2 * c) & (4 * c + to != 7)
        return wanted, remote(
            kr.at[jnp.clip(to - 1 + c, 0, 2), at: at + CHUNK], xr.at[k - 1, at: at + CHUNK],
            px_s.at[i, k - 1], px_r.at[i, k - 1], to * NC + c, s,
        )

    def weight_sum(i):
        at = CHUNK * i
        arrived(crv.at[:, at: at + CHUNK], pc_s.at[i], pc_r.at[i])
        kr[:, at: at + CHUNK] = (
            pw[pl.ds(1 + 3 * c, 3), at: at + CHUNK].astype(F32)
            + crv[:, at: at + CHUNK].astype(F32)
        ).astype(BF16)
        for k in range(1, NX):
            wanted, copy = late_to(i, k)
            pl.when(wanted)(copy.start)

    def weight_z(i, blocks):
        at = CHUNK * i

        @pl.when(late)
        def _():
            for k in range(1, NX):
                arrived(xr.at[k - 1, at: at + CHUNK], px_s.at[i, k - 1], px_r.at[i, k - 1])

        if i == 0:
            @pl.when(early)
            def _():
                for k in range(1, NX):
                    arrived(xr.at[k - 1], pxe_s, pxe_r.at[k - 1])

        total = jnp.where(
            early, kre[at: at + CHUNK].astype(F32),
            kr[jnp.clip(x - 1 + c, 0, 2), at: at + CHUNK].astype(F32),
        )
        for k in range(1, NX):
            total = total + xr[k - 1, at: at + CHUNK].astype(F32)
        total = jnp.where(early | late, total, 0.0)
        zr[at: at + CHUNK] = total.astype(BF16)
        for b in blocks:
            @pl.when(z != b)
            def _():
                remote(
                    zr.at[BLOCK * b: BLOCK * b + BLOCK], zb.at[z],
                    pz_s.at[b], pz_r.at[z], dp, b * NY + y,
                ).start()

    def back_sum(i):
        for k in range(1, NY):
            arrived(gr.at[i, k - 1], gy_s.at[i, k - 1], gy_r.at[i, k - 1])
        total = gs[i, :, y].astype(F32)
        for k in range(1, NY):
            total = total + gr[i, k - 1].astype(F32)
        gz[i] = total.astype(BF16)
        for k in Z_ORDER:
            to = at_z(k)
            send(
                gz.at[i, to], gf.at[i, z], gz_s.at[i, k - 1], gz_r.at[i, k - 1], dp, to * NY + y
            )
        gf[i, z] = gz[i, z]

    def back_done(i):
        at = CHUNK * i
        for k in Z_ORDER:
            arrived(gf.at[i, at_z(-k)], gz_s.at[i, k - 1], gz_r.at[i, k - 1])
        grad[:, at: at + CHUNK] = (
            cot[:, at: at + CHUNK].astype(F32) + gf[i].reshape(128, CHUNK).astype(F32)
        ).astype(BF16)

    def spatial_backward(group):
        at = 256 * group
        q, k, v = (qkv[:, at + WIDTH * i: at + WIDTH * i + 384] for i in range(3))
        probs = [prs[2 * group + j] for j in range(2)]
        grads = backward4(grad[:, at: at + 384], q, k, v, probs, head_masks(32 * group))
        for i in range(3):
            acc[:, at + WIDTH * i: at + WIDTH * i + 384] += grads[i]

    def out_z():
        for k in range(1, NY):
            arrived(ty.at[at_y(-k)], ty_s.at[k - 1], ty_r.at[k - 1])
        whole = [None] * 9
        for i in range(NY):
            for t in range(3):
                tile = ty[i, :, :, 128 * t: 128 * t + 128].astype(F32)
                at = 2 * i + t
                whole[at] = tile if whole[at] is None else whole[at] + tile
        for t in range(9):
            tw[:, :, 128 * t: 128 * t + 128] = whole[t].astype(BF16)
        for k in Z_ORDER:
            to = at_z(k)
            send(tw.at[to], tf.at[z], tz_s.at[k - 1], tz_r.at[k - 1], dp, to * NY + y)
        tf[z] = tw[z]

    def final_y():
        zb[z] = zr[pl.ds(m16(BLOCK * z), BLOCK)]
        for b in range(NZ):
            @pl.when(z != b)
            def _():
                arrived(zb.at[b], pz_s.at[b], pz_r.at[b])
        total = zb[0].astype(F32)
        for i in range(1, NZ):
            total = total + zb[i].astype(F32)
        fr[0:BLOCK, :] = total
        fr[BLOCK:160, :] = jnp.zeros((16, 128), F32)
        for i in range(NY):
            fs[i] = fr[36 * i: 36 * i + 48, :].astype(BF16)
        for k in range(1, NY):
            to = at_y(k)
            send(fs.at[to], fy.at[y], py_s.at[k - 1], py_r.at[k - 1], dp, z * NY + to)
        fy[y] = fs[y]

    def moves(tile):
        return [
            (g, d) for g in range(NY) for d in placed(g, tile) if d != tile_owner(tile)
        ]

    def move(tile, g, d):
        return remote(
            fy.at[g], fd.at[OWNER[tile], g], pd_s.at[g, d], pd_r.at[tile, g], d, s
        )

    def final_dp():
        for k in range(1, NY):
            arrived(fy.at[at_y(-k)], py_s.at[k - 1], py_r.at[k - 1])
        for tile in range(7):
            @pl.when(dp == tile_owner(tile))
            def _():
                for g, d in moves(tile):
                    move(tile, g, d).start()
        fd[mine] = fy[...]

    weight_chunk(0)
    back_chunk(0)
    weight_chunk(1)
    weight_sum(0)
    weight_chunk(2)
    weight_sum(1)
    back_chunk(1)
    weight_sum(2)
    back_chunk(2)
    out_z()
    acc[...] = jnp.zeros_like(acc)
    weight_z(0, (0, 1))
    back_sum(0)
    weight_z(1, (2, 3, 4))
    back_sum(1)
    weight_z(2, (5, 6, 7))
    back_sum(2)
    back_done(0)
    spatial_backward(0)
    final_y()
    back_done(1)
    spatial_backward(1)
    final_dp()
    back_done(2)
    spatial_backward(2)
    spatial_backward(3)
    gqkv[...] = acc[...].astype(BF16)
    for k in Z_ORDER:
        arrived(tf.at[at_z(-k)], tz_s.at[k - 1], tz_r.at[k - 1])
    bo[...] = (sob[...].astype(F32) + tf[...].reshape(128, WIDTH).astype(F32)).astype(BF16)

    for d in range(NX * NC):
        @pl.when(dp == d)
        def _():
            for tile in range(7):
                for g, to in moves(tile):
                    if to == d:
                        arrived(fd.at[OWNER[tile], g], pd_s.at[g, d], pd_r.at[tile, g])
    gwf[...] = jnp.zeros_like(gwf)
    lane = lax.broadcasted_iota(jnp.int32, (48, 384), 1)
    for g in range(NY):
        for i in range(3):
            window = jnp.concatenate(
                [fd[OWNER[2 * i + t], g].astype(F32) for t in range(3)], axis=1
            )
            if i > 0:
                window = pltpu.roll(window, 384 - 32 * i, 1)
            window = jnp.where(lane < 288, window, 0.0)
            if g > 0:
                window = pltpu.roll(window, 32 * g, 1)
            at = PART_AT[i] + 256 * g
            gwf[:, at: at + 384] += window
    picked = jnp.zeros((48, 432), F32)
    for d in range(NX * NC):
        picked = jnp.where(dp == d, gwf[:, 432 * d: 432 * d + 432], picked)
    gw[...] = picked[0:36].astype(BF16)

    for copy in sent:
        copy.wait_send()

    @pl.when(x != 2 * c)
    def _():
        early_to().wait_send()

    for i in range(3):
        for k in range(1, NX):
            wanted, copy = late_to(i, k)
            pl.when(wanted)(copy.wait_send)
    for b in range(NZ):
        @pl.when(z != b)
        def _():
            remote(
                zr.at[BLOCK * b: BLOCK * b + BLOCK], zb.at[z], pz_s.at[b], pz_r.at[z], dp, s
            ).wait_send()
    for tile in range(7):
        @pl.when(dp == tile_owner(tile))
        def _():
            for g, d in moves(tile):
                move(tile, g, d).wait_send()


def local(spatial_qkv, lengths, w_qkv, cotangent):
    frames, patches = spatial_qkv.shape[1], spatial_qkv.shape[2]
    vmem = pl.BlockSpec(memory_space=pltpu.VMEM)
    hbm = pl.BlockSpec(memory_space=pltpu.HBM)
    dma = pltpu.SemaphoreType.DMA

    def bf(*shape):
        return pltpu.VMEM(shape, BF16)

    def fl(*shape):
        return pltpu.VMEM(shape, F32)

    out = pl.pallas_call(
        kernel,
        out_shape=(
            jax.ShapeDtypeStruct((patches, WIDTH), BF16),
            jax.ShapeDtypeStruct((patches, 3 * WIDTH), BF16),
            jax.ShapeDtypeStruct((36, 432), BF16),
        ),
        in_specs=[pl.BlockSpec(memory_space=pltpu.SMEM), hbm, vmem, hbm],
        out_specs=(vmem, vmem, vmem),
        scratch_shapes=[
            bf(128, 3 * WIDTH),
            bf(128, WIDTH),
            fl(128, 3 * WIDTH),
            fl(8, 128, 256),
            fl(4, 2, 128, 256),
            bf(4, 4, 128, 384),
            bf(128, WIDTH),
            bf(4, 8, 48, 128),
            bf(4, 48, 128),
            fl(160, 128),
            bf(8, WIDTH, 128),
            bf(8, 4, 16, WIDTH),
            bf(4, 128, 384),
            bf(8, 4, 16, 384),
            fl(3, 512, 128),
            fl(7, 512, 128),
            fl(3, 512, 128),
            bf(8, 4, 16, 384),
            bf(4, 8, 16, 384),
            bf(8, 16, WIDTH),
            bf(8, 16, WIDTH),
            fl(7, 512, 128),
            bf(512, 1024),
            bf(3, 8, 4, 16, CHUNK),
            bf(3, 3, 8, 16, CHUNK),
            bf(3, 8, 16, CHUNK),
            bf(3, 8, 16, CHUNK),
            bf(128, WIDTH),
            bf(8, WIDTH, 128),
            fl(4, 128, 128),
            bf(WIDTH, 128),
            bf(WIDTH, 128),
            bf(3, WIDTH, 128),
            bf(3, WIDTH, 128),
            bf(3, WIDTH, 128),
            bf(WIDTH, 128),
            bf(8, BLOCK, 128),
            fl(160, 128),
            bf(4, 48, 128),
            bf(4, 48, 128),
            bf(8, 4, 48, 128),
            fl(48, 3 * WIDTH),
            dma((2,)), dma((3,)), dma((3,)), dma((7,)), dma((7,)),
            dma((8, 3)), dma((8, 3)), dma((8,)), dma((8,)),
            dma((3,)), dma((3,)), dma((7,)), dma((7,)),
            dma((7,)), dma((7,)), dma((8, 3)), dma((8, 3)),
            dma((3,)), dma((3,)), dma((7,)), dma((7,)),
            dma((3, 3)), dma((3, 3)), dma((3, 7)), dma((3, 7)),
            dma, dma, dma, dma((3,)),
            dma((3,)), dma((3,)), dma((3, 3)), dma((3, 3)), dma((8,)), dma((8,)),
            dma((3,)), dma((3,)), dma((4, 8)), dma((8, 4)),
        ],
        compiler_params=pltpu.CompilerParams(
            collective_id=0, has_side_effects=True, vmem_limit_bytes=52 * 1024 * 1024
        ),
    )(
        lengths, spatial_qkv.reshape(patches, 3 * WIDTH), w_qkv,
        cotangent.reshape(patches, WIDTH),
    )
    return (
        out[0].reshape(1, frames, patches, WIDTH),
        out[1].reshape(1, frames, patches, 3 * WIDTH),
        out[2],
    )


def solution(mesh):
    in_specs = (P("dp", "seq", None, None), P("dp"), P("seq", None), P("dp", "seq", None, None))
    out_specs = (P("dp", "seq", None, None), P("dp", "seq", None, None), P("seq", "dp"))
    return jax.shard_map(local, mesh=mesh, in_specs=in_specs, out_specs=out_specs, check_vma=False)
```

```python
import jax
import jax.numpy as jnp
from jax import lax
from jax.experimental import pallas as pl
from jax.experimental.pallas import tpu as pltpu
from jax.sharding import PartitionSpec as P

HEADS = 16
WIDTH = 1152
HEAD = 72
NY, NZ, NX, NC = 4, 8, 4, 2
MESH = pl.DeviceIdType.MESH
F32, BF16 = jnp.float32, jnp.bfloat16
SCALE = HEAD ** (-0.5)


def dot(a, b):
    return lax.dot_general(a, b, (((1,), (0,)), ((), ())), preferred_element_type=F32)


def dot_nt(a, b):
    return lax.dot_general(a, b, (((1,), (1,)), ((), ())), preferred_element_type=F32)


def dot_tn(a, b):
    return lax.dot_general(a, b, (((0,), (0,)), ((), ())), preferred_element_type=F32)


def half(window, pair):
    return window[:, 0:256] if pair == 0 else window[:, 128:384]


def head_masks(off):
    lane = lax.broadcasted_iota(jnp.int32, (128, 256), 1)
    masks = []
    for j in range(4):
        low = off + HEAD * j - (128 if j >= 2 else 0)
        masks.append(jnp.where((lane >= low) & (lane < low + HEAD), 1.0, 0.0).astype(BF16))
    return masks


def two(window, pair, masks):
    own = half(window, pair)
    return jnp.concatenate([own * masks[2 * pair], own * masks[2 * pair + 1]], axis=0)


def stack(array):
    return jnp.concatenate([array[:, 0:128], array[:, 128:256]], axis=0)


def join(parts):
    left, right = parts
    return jnp.concatenate(
        [left[:, 0:128], left[:, 128:256] + right[:, 0:128], right[:, 128:256]], axis=1
    )


def forward4(q, k, v, masks, live):
    probs, outs = [], []
    for pair in range(2):
        scores = dot_nt(half(k, pair), two(q, pair, masks)) * SCALE
        if live is not None:
            scores = jnp.where(live, scores, -1e30)
        expo = jnp.exp(scores - jnp.max(scores, axis=0, keepdims=True))
        prob = expo * (1.0 / jnp.sum(expo, axis=0, keepdims=True))
        probs.append(prob)
        outs.append(dot_tn(stack(prob.astype(BF16)), two(v, pair, masks)))
    return join(outs), probs


def backward4(g, q, k, v, probs, masks, values=True):
    dqs, dks, dvs = [], [], []
    for pair in range(2):
        prob = probs[pair]
        g_two = two(g, pair, masks)
        if values:
            dvs.append(dot(prob.astype(BF16), g_two))
        gp = dot_nt(half(v, pair), g_two)
        gs = prob * (gp - jnp.sum(gp * prob, axis=0, keepdims=True))
        low = (gs * SCALE).astype(BF16)
        dqs.append(dot_tn(stack(low), two(k, pair, masks)))
        dks.append(dot(low, two(q, pair, masks)))
    return (join(dqs), join(dks)) + ((join(dvs),) if values else ())


def remote(src, dst, ssem, rsem, dp, s):
    return pltpu.make_async_remote_copy(
        src_ref=src, dst_ref=dst, send_sem=ssem, recv_sem=rsem,
        device_id=(dp, s), device_id_type=MESH,
    )


def m16(value):
    return pl.multiple_of(value, 16)


Z_ORDER = (1, 7, 2, 6, 3, 5, 4)
BLOCK = 144
CHUNK = 384


PART_AT = (2 * WIDTH, 0, WIDTH)
OWNER = (0, 6, 1, 2, 3, 4, 5, 7)


def placed(group, tile):
    found = set()
    for part in range(3):
        low = max(128 * tile, 288 * part)
        high = min(128 * tile + 128, 288 * part + 288)
        if low < high:
            shift = PART_AT[part] + 288 * group - 288 * part
            found |= set(range((low + shift) // 432, (high - 1 + shift) // 432 + 1))
    return sorted(found)


def tile_owner(tile):
    return 2 * (OWNER[tile] % 4) + OWNER[tile] // 4


def kernel(
    len_ref, qkv_h, w, cot_h, bo, gqkv, gw,
    qkv, cot, acc, prs, prt, blk, sob, wp, wr, wm, wf, so, cy, cz, c32, pj, to32, tob, ty, tw, tf,
    gp32, gpb, gs, gr, gz, gf, grad, pw, dv2, cre, kre, crv, kr, xr, zr, zb, fr, fs, fy, fd, gwf,
    in_s, wy_s, wy_r, wz_s, wz_r, wx_s, wx_r, wd_s, wd_r, cy_s, cy_r, cz_s, cz_r,
    sz_s, sz_r, sy_s, sy_r, ty_s, ty_r, tz_s, tz_r, gy_s, gy_r, gz_s, gz_r,
    pe_s, pe_r, pxe_s, pxe_r, pc_s, pc_r, px_s, px_r, pz_s, pz_r, py_s, py_r, pd_s, pd_r,
):
    dp, s = lax.axis_index("dp"), lax.axis_index("seq")
    y, z = lax.rem(s, NY), lax.div(s, NY)
    c, x = lax.rem(dp, NC), lax.div(dp, NC)
    sib = x * NC + (1 - c)
    mine = 4 * c + x
    sent = []

    def at_y(k):
        return lax.rem(y + k + NY, NY)

    def at_z(k):
        return lax.rem(z + k + NZ, NZ)

    def at_x(k):
        return lax.rem(x + k + NX, NX)

    def send(src, dst, ssem, rsem, dp_to, s_to):
        copy = remote(src, dst, ssem, rsem, dp_to, s_to)
        copy.start()
        sent.append(copy)

    def arrived(dst, ssem, rsem):
        remote(dst, dst, ssem, rsem, dp, s).wait_recv()

    barrier = pltpu.get_barrier_semaphore()
    for k in range(1, NY):
        pl.semaphore_signal(barrier, inc=1, device_id=(dp, z * NY + at_y(k)), device_id_type=MESH)
    for k in range(1, NZ):
        pl.semaphore_signal(barrier, inc=1, device_id=(dp, at_z(k) * NY + y), device_id_type=MESH)
    for k in range(1, NX * NC):
        pl.semaphore_signal(
            barrier, inc=1, device_id=(lax.rem(dp + k, NX * NC), s), device_id_type=MESH
        )
    qkv_in = pltpu.make_async_copy(qkv_h, qkv, in_s.at[0])
    cot_in = pltpu.make_async_copy(cot_h, cot, in_s.at[1])
    qkv_in.start()
    cot_in.start()

    wrow = w[...].astype(F32)
    for g in range(NY):
        piece = jnp.concatenate(
            [wrow[:, 288 * g + at: 288 * g + at + 288] for at in PART_AT]
            + [jnp.zeros((36, 160), F32)], axis=1
        )
        piece = jnp.concatenate([piece, jnp.zeros((12, 1024), F32)], axis=0).astype(BF16)
        for t in range(8):
            wp[g, OWNER[t]] = piece[:, 128 * t: 128 * t + 128]
    wr[y] = wp[y, mine]

    def spatial_forward(group):
        at = pl.multiple_of(256 * group, 128)
        q, k, v = (qkv[:, pl.ds(at + WIDTH * i, 384)] for i in range(3))
        out, probs = forward4(q, k, v, head_masks(32 * group), None)
        acc[:, pl.ds(at, 384)] += out
        for j in range(2):
            prs[2 * group + j] = probs[j]


    pl.semaphore_wait(barrier, NY + NZ + NX * NC - 3)
    for k in range(1, NY):
        to = at_y(k)
        send(wp.at[to, mine], wr.at[y], wy_s.at[k - 1], wy_r.at[k - 1], dp, z * NY + to)
    acc[...] = jnp.zeros_like(acc)
    fd[...] = jnp.zeros_like(fd)
    cot_in.wait()
    cy[y] = cot[:, pl.ds(pl.multiple_of(256 * y, 128), 384)]
    for k in range(1, NY):
        to = at_y(k)
        send(
            cot.at[:, pl.ds(pl.multiple_of(256 * to, 128), 384)], cy.at[y],
            cy_s.at[k - 1], cy_r.at[k - 1], dp, z * NY + to,
        )

    qkv_in.wait()
    for group in range(4):
        spatial_forward(group)
    sob[...] = acc[:, 0:WIDTH].astype(BF16)
    so[z, y] = sob[pl.ds(m16(16 * z), 16), :]

    for k in range(1, NY):
        arrived(wr.at[at_y(-k)], wy_s.at[k - 1], wy_r.at[k - 1])
    for i in range(NY):
        wm[36 * i: 36 * i + 48, :] = wr[i].astype(F32)
    wf[mine, pl.ds(m16(BLOCK * z), BLOCK)] = wm[0:BLOCK, :].astype(BF16)

    def rows(k):
        return pl.ds(m16(BLOCK * at_z(k)), BLOCK)

    def weight_x(order, k):
        for i in range(1, NX):
            block = wf.at[mine, rows(k)]
            send(block, block, wx_s.at[order, i - 1], wx_r.at[order, i - 1], at_x(i) * NC + c, s)

    def spread_y(order, k):
        for i in range(1, NY):
            block = so.at[at_z(k), y]
            send(block, block, sy_s.at[order, i - 1], sy_r.at[order, i - 1], dp, z * NY + at_y(i))

    def weight_on(k, step, way):
        block = wf.at[mine, rows(k)]
        send(block, block, wz_s.at[way - 1], wz_r.at[way - 1], dp, at_z(step) * NY + y)

    for k in (1, 7, 2, 6):
        weight_on(0, k, k)
    weight_x(0, 0)
    for k in Z_ORDER:
        to = at_z(k)
        send(
            sob.at[pl.ds(m16(16 * to), 16)], so.at[z, y],
            sz_s.at[k - 1], sz_r.at[k - 1], dp, to * NY + y,
        )
    spread_y(0, 0)
    for order, k in enumerate(Z_ORDER):
        arrived(wf.at[mine, rows(-k)], wz_s.at[k - 1], wz_r.at[k - 1])
        if k == 2:
            weight_on(-2, 1, 3)
            weight_on(-2, 2, 4)
        if k == 6:
            weight_on(2, -1, 5)
        weight_x(order + 1, -k)
        arrived(so.at[at_z(-k), y], sz_s.at[k - 1], sz_r.at[k - 1])
        spread_y(order + 1, -k)

    for k in range(1, NY):
        arrived(cy.at[at_y(-k)], cy_s.at[k - 1], cy_r.at[k - 1])
    for k in Z_ORDER:
        to = at_z(k)
        send(
            cy.at[:, pl.ds(m16(16 * to), 16)], cz.at[z],
            cz_s.at[k - 1], cz_r.at[k - 1], dp, to * NY + y,
        )
    cz[z] = cy[:, pl.ds(m16(16 * z), 16), :]

    for order, k in enumerate((0,) + Z_ORDER):
        for i in range(1, NX):
            arrived(
                wf.at[4 * c + at_x(-i), rows(-k)], wx_s.at[order, i - 1], wx_r.at[order, i - 1]
            )
        block = wf.at[pl.ds(4 * c, 4), rows(-k)]
        send(block, block, wd_s.at[order], wd_r.at[order], sib, s)
    for order, k in enumerate((0,) + Z_ORDER):
        for i in range(1, NY):
            arrived(so.at[at_z(-k), at_y(-i)], sy_s.at[order, i - 1], sy_r.at[order, i - 1])
    for order, k in enumerate((0,) + Z_ORDER):
        arrived(wf.at[pl.ds(4 - 4 * c, 4), rows(-k)], wd_s.at[order], wd_r.at[order])

    every = so[...].reshape(512, WIDTH)
    for t in range(4):
        if t < 3:
            pair = dot(
                every, jnp.concatenate([wf[OWNER[2 * t]], wf[OWNER[2 * t + 1]]], axis=1)
            )
            pj[2 * t], pj[2 * t + 1] = pair[:, 0:128], pair[:, 128:256]
        else:
            pj[6] = dot(every, wf[OWNER[6]])

    length = len_ref[0]
    key = lax.broadcasted_iota(jnp.int32, (128, 256), 0)
    query = lax.broadcasted_iota(jnp.int32, (128, 256), 1) & 127
    live = ((key >> 5) == (query >> 5)) & ((key & 31) < length)
    masks = head_masks(0)

    def rows_of(ref, first, b):
        return jnp.concatenate(
            [
                jnp.concatenate(
                    [ref[t, pl.ds(4 * b + i, 32, stride=16), :] for i in range(4)], axis=0
                )
                for t in range(first, first + 3)
            ],
            axis=1,
        )

    def temporal_forward(b, carry):
        v = rows_of(pj, 0, b).astype(BF16)
        q = pltpu.roll(rows_of(pj, 2, b), 384 - 32, 1).astype(BF16)
        k = pltpu.roll(rows_of(pj, 4, b), 384 - 64, 1).astype(BF16)
        blk[b, 0], blk[b, 1], blk[b, 2] = q, k, v
        out, probs = forward4(q, k, v, masks, live)
        for j in range(2):
            prt[b, j] = probs[j]
        for i in range(4):
            for t in range(3):
                to32[t, pl.ds(4 * b + i, 32, stride=16), :] = out[
                    32 * i: 32 * i + 32, 128 * t: 128 * t + 128
                ]
        return carry

    for b in range(0, 4):
        temporal_forward(b, 0)

    t_out = jnp.concatenate([to32[t] for t in range(3)], axis=1)
    turned = t_out
    for k in range(1, NY):
        turned = jnp.where(y == k, pltpu.roll(t_out, 32 * k, 1), turned)
    tob[...] = turned.astype(BF16).reshape(NZ, NY, 16, 384)
    for k in range(1, NY):
        to = at_y(k)
        send(tob.at[:, to], ty.at[y], ty_s.at[k - 1], ty_r.at[k - 1], dp, z * NY + to)
    ty[y] = tob[:, y]

    for k in Z_ORDER:
        arrived(cz.at[at_z(-k)], cz_s.at[k - 1], cz_r.at[k - 1])
    g_in = cz[...].reshape(512, 384).astype(F32)
    turned = g_in
    for k in range(1, NY):
        turned = jnp.where(y == k, pltpu.roll(g_in, 384 - 32 * k, 1), turned)
    for t in range(3):
        c32[t] = turned[:, 128 * t: 128 * t + 128]

    def scatter(ref, first, b, array):
        for i in range(4):
            for t in range(array.shape[1] // 128):
                ref[first + t, pl.ds(4 * b + i, 32, stride=16), :] = array[
                    32 * i: 32 * i + 32, 128 * t: 128 * t + 128
                ]

    def temporal_values(b, carry):
        g = rows_of(c32, 0, b).astype(BF16)
        blk[b, 3] = g
        dv = join([
            dot(prt[b, pair].astype(BF16), two(g, pair, masks)) for pair in range(2)
        ])
        scatter(gp32, 0, b, dv[:, 0:256])
        dv2[b] = dv[:, 256:384]
        return carry

    def temporal_backward(b, carry):
        q, k, v, g = blk[b, 0], blk[b, 1], blk[b, 2], blk[b, 3]
        dq, dk = backward4(g, q, k, v, [prt[b, j] for j in range(2)], masks, False)
        dq, dk = pltpu.roll(dq, 32, 1), pltpu.roll(dk, 64, 1)
        packed = jnp.concatenate(
            [dv2[b] + dq[:, 0:128], dq[:, 128:256], dq[:, 256:384] + dk[:, 0:128], dk[:, 128:384]],
            axis=1,
        )
        scatter(gp32, 2, b, packed)
        return carry

    def weight_part(at, low, high):
        part = dot_tn(
            so[:, :, :, at: at + CHUNK].reshape(512, CHUNK), gpb[:, 128 * low: 128 * high]
        ).astype(BF16)
        for t in range(low, high):
            pw[OWNER[t], at: at + CHUNK] = part[:, 128 * (t - low): 128 * (t - low) + 128]

    early, late = x == 2 * c, (x != 2 * c) & (mine != 7)

    def early_weight():
        for i in range(3):
            weight_part(CHUNK * i, 0, 2)
        send(pw.at[6 - 6 * c], cre, pe_s, pe_r, sib, s)

    def early_to():
        k = lax.rem(2 * c - x + NX, NX)
        slot = jnp.maximum(k - 1, 0)
        return remote(
            kre, xr.at[slot], pxe_s, pxe_r.at[slot], 2 * c * NC + c, s
        )

    def early_sum():
        arrived(cre, pe_s, pe_r)
        kre[...] = (pw[6 * c].astype(F32) + cre[...].astype(F32)).astype(BF16)

        @pl.when(x != 2 * c)
        def _():
            early_to().start()

    for b in range(0, 4):
        temporal_values(b, 0)
    for t in range(2):
        gpb[:, 128 * t: 128 * t + 128] = gp32[t].astype(BF16)
    early_weight()
    for b in range(0, 2):
        temporal_backward(b, 0)
    early_sum()
    for b in range(2, 4):
        temporal_backward(b, 0)
    for t in range(2, 7):
        gpb[:, 128 * t: 128 * t + 128] = gp32[t].astype(BF16)

    def weight_chunk(i):
        at = CHUNK * i
        weight_part(at, 2, 7)
        send(
            pw.at[pl.ds(4 - 3 * c, 3), at: at + CHUNK], crv.at[:, at: at + CHUNK],
            pc_s.at[i], pc_r.at[i], sib, s,
        )

    def back_chunk(i):
        at = CHUNK * i
        part = jnp.zeros((512, CHUNK), F32)
        for t in range(4):
            if t < 3:
                weight = jnp.concatenate(
                    [wf[OWNER[2 * t], at: at + CHUNK], wf[OWNER[2 * t + 1], at: at + CHUNK]],
                    axis=1,
                )
                part = part + dot_nt(gpb[:, 256 * t: 256 * t + 256], weight)
            else:
                part = part + dot_nt(gpb[:, 768:896], wf[OWNER[6], at: at + CHUNK])
        gs[i] = part.astype(BF16).reshape(NZ, NY, 16, CHUNK)
        for k in range(1, NY):
            to = at_y(k)
            send(
                gs.at[i, :, to], gr.at[i, k - 1],
                gy_s.at[i, k - 1], gy_r.at[i, k - 1], dp, z * NY + to,
            )

    def late_to(i, k):
        at = CHUNK * i
        to = at_x(k)
        wanted = (to != 2 * c) & (4 * c + to != 7)
        return wanted, remote(
            kr.at[jnp.clip(to - 1 + c, 0, 2), at: at + CHUNK], xr.at[k - 1, at: at + CHUNK],
            px_s.at[i, k - 1], px_r.at[i, k - 1], to * NC + c, s,
        )

    def weight_sum(i):
        at = CHUNK * i
        arrived(crv.at[:, at: at + CHUNK], pc_s.at[i], pc_r.at[i])
        kr[:, at: at + CHUNK] = (
            pw[pl.ds(1 + 3 * c, 3), at: at + CHUNK].astype(F32)
            + crv[:, at: at + CHUNK].astype(F32)
        ).astype(BF16)
        for k in range(1, NX):
            wanted, copy = late_to(i, k)
            pl.when(wanted)(copy.start)

    def weight_z(i, blocks):
        at = CHUNK * i

        @pl.when(late)
        def _():
            for k in range(1, NX):
                arrived(xr.at[k - 1, at: at + CHUNK], px_s.at[i, k - 1], px_r.at[i, k - 1])

        if i == 0:
            @pl.when(early)
            def _():
                for k in range(1, NX):
                    arrived(xr.at[k - 1], pxe_s, pxe_r.at[k - 1])

        total = jnp.where(
            early, kre[at: at + CHUNK].astype(F32),
            kr[jnp.clip(x - 1 + c, 0, 2), at: at + CHUNK].astype(F32),
        )
        for k in range(1, NX):
            total = total + xr[k - 1, at: at + CHUNK].astype(F32)
        total = jnp.where(early | late, total, 0.0)
        zr[at: at + CHUNK] = total.astype(BF16)
        for b in blocks:
            @pl.when(z != b)
            def _():
                remote(
                    zr.at[BLOCK * b: BLOCK * b + BLOCK], zb.at[z],
                    pz_s.at[b], pz_r.at[z], dp, b * NY + y,
                ).start()

    def back_sum(i):
        for k in range(1, NY):
            arrived(gr.at[i, k - 1], gy_s.at[i, k - 1], gy_r.at[i, k - 1])
        total = gs[i, :, y].astype(F32)
        for k in range(1, NY):
            total = total + gr[i, k - 1].astype(F32)
        gz[i] = total.astype(BF16)
        for k in Z_ORDER:
            to = at_z(k)
            send(
                gz.at[i, to], gf.at[i, z], gz_s.at[i, k - 1], gz_r.at[i, k - 1], dp, to * NY + y
            )
        gf[i, z] = gz[i, z]

    def back_done(i):
        at = CHUNK * i
        for k in Z_ORDER:
            arrived(gf.at[i, at_z(-k)], gz_s.at[i, k - 1], gz_r.at[i, k - 1])
        grad[:, at: at + CHUNK] = (
            cot[:, at: at + CHUNK].astype(F32) + gf[i].reshape(128, CHUNK).astype(F32)
        ).astype(BF16)

    def spatial_backward(group):
        at = 256 * group
        q, k, v = (qkv[:, at + WIDTH * i: at + WIDTH * i + 384] for i in range(3))
        probs = [prs[2 * group + j] for j in range(2)]
        grads = backward4(grad[:, at: at + 384], q, k, v, probs, head_masks(32 * group))
        for i in range(3):
            acc[:, at + WIDTH * i: at + WIDTH * i + 384] += grads[i]

    def out_z():
        for k in range(1, NY):
            arrived(ty.at[at_y(-k)], ty_s.at[k - 1], ty_r.at[k - 1])
        whole = [None] * 9
        for i in range(NY):
            for t in range(3):
                tile = ty[i, :, :, 128 * t: 128 * t + 128].astype(F32)
                at = 2 * i + t
                whole[at] = tile if whole[at] is None else whole[at] + tile
        for t in range(9):
            tw[:, :, 128 * t: 128 * t + 128] = whole[t].astype(BF16)
        for k in Z_ORDER:
            to = at_z(k)
            send(tw.at[to], tf.at[z], tz_s.at[k - 1], tz_r.at[k - 1], dp, to * NY + y)
        tf[z] = tw[z]

    def final_y():
        zb[z] = zr[pl.ds(m16(BLOCK * z), BLOCK)]
        for b in range(NZ):
            @pl.when(z != b)
            def _():
                arrived(zb.at[b], pz_s.at[b], pz_r.at[b])
        total = zb[0].astype(F32)
        for i in range(1, NZ):
            total = total + zb[i].astype(F32)
        fr[0:BLOCK, :] = total
        fr[BLOCK:160, :] = jnp.zeros((16, 128), F32)
        for i in range(NY):
            fs[i] = fr[36 * i: 36 * i + 48, :].astype(BF16)
        for k in range(1, NY):
            to = at_y(k)
            send(fs.at[to], fy.at[y], py_s.at[k - 1], py_r.at[k - 1], dp, z * NY + to)
        fy[y] = fs[y]

    def moves(tile):
        return [
            (g, d) for g in range(NY) for d in placed(g, tile) if d != tile_owner(tile)
        ]

    def move(tile, g, d):
        return remote(
            fy.at[g], fd.at[OWNER[tile], g], pd_s.at[g, d], pd_r.at[tile, g], d, s
        )

    def final_dp():
        for k in range(1, NY):
            arrived(fy.at[at_y(-k)], py_s.at[k - 1], py_r.at[k - 1])
        for tile in range(7):
            @pl.when(dp == tile_owner(tile))
            def _():
                for g, d in moves(tile):
                    move(tile, g, d).start()
        fd[mine] = fy[...]

    weight_chunk(0)
    back_chunk(0)
    weight_chunk(1)
    weight_sum(0)
    out_z()
    weight_chunk(2)
    weight_sum(1)
    back_chunk(1)
    weight_sum(2)
    back_chunk(2)
    acc[...] = jnp.zeros_like(acc)
    weight_z(0, (0, 1))
    back_sum(0)
    weight_z(1, (2, 3, 4))
    back_sum(1)
    weight_z(2, (5, 6, 7))
    back_sum(2)
    back_done(0)
    spatial_backward(0)
    final_y()
    back_done(1)
    spatial_backward(1)
    final_dp()
    back_done(2)
    spatial_backward(2)
    spatial_backward(3)
    gqkv[...] = acc[...].astype(BF16)
    for k in Z_ORDER:
        arrived(tf.at[at_z(-k)], tz_s.at[k - 1], tz_r.at[k - 1])
    bo[...] = (sob[...].astype(F32) + tf[...].reshape(128, WIDTH).astype(F32)).astype(BF16)

    for d in range(NX * NC):
        @pl.when(dp == d)
        def _():
            for tile in range(7):
                for g, to in moves(tile):
                    if to == d:
                        arrived(fd.at[OWNER[tile], g], pd_s.at[g, d], pd_r.at[tile, g])
    gwf[...] = jnp.zeros_like(gwf)
    lane = lax.broadcasted_iota(jnp.int32, (48, 384), 1)
    for g in range(NY):
        for i in range(3):
            window = jnp.concatenate(
                [fd[OWNER[2 * i + t], g].astype(F32) for t in range(3)], axis=1
            )
            if i > 0:
                window = pltpu.roll(window, 384 - 32 * i, 1)
            window = jnp.where(lane < 288, window, 0.0)
            if g > 0:
                window = pltpu.roll(window, 32 * g, 1)
            at = PART_AT[i] + 256 * g
            gwf[:, at: at + 384] += window
    picked = jnp.zeros((48, 432), F32)
    for d in range(NX * NC):
        picked = jnp.where(dp == d, gwf[:, 432 * d: 432 * d + 432], picked)
    gw[...] = picked[0:36].astype(BF16)

    for copy in sent:
        copy.wait_send()

    @pl.when(x != 2 * c)
    def _():
        early_to().wait_send()

    for i in range(3):
        for k in range(1, NX):
            wanted, copy = late_to(i, k)
            pl.when(wanted)(copy.wait_send)
    for b in range(NZ):
        @pl.when(z != b)
        def _():
            remote(
                zr.at[BLOCK * b: BLOCK * b + BLOCK], zb.at[z], pz_s.at[b], pz_r.at[z], dp, s
            ).wait_send()
    for tile in range(7):
        @pl.when(dp == tile_owner(tile))
        def _():
            for g, d in moves(tile):
                move(tile, g, d).wait_send()


def local(spatial_qkv, lengths, w_qkv, cotangent):
    frames, patches = spatial_qkv.shape[1], spatial_qkv.shape[2]
    vmem = pl.BlockSpec(memory_space=pltpu.VMEM)
    hbm = pl.BlockSpec(memory_space=pltpu.HBM)
    dma = pltpu.SemaphoreType.DMA

    def bf(*shape):
        return pltpu.VMEM(shape, BF16)

    def fl(*shape):
        return pltpu.VMEM(shape, F32)

    out = pl.pallas_call(
        kernel,
        out_shape=(
            jax.ShapeDtypeStruct((patches, WIDTH), BF16),
            jax.ShapeDtypeStruct((patches, 3 * WIDTH), BF16),
            jax.ShapeDtypeStruct((36, 432), BF16),
        ),
        in_specs=[pl.BlockSpec(memory_space=pltpu.SMEM), hbm, vmem, hbm],
        out_specs=(vmem, vmem, vmem),
        scratch_shapes=[
            bf(128, 3 * WIDTH),
            bf(128, WIDTH),
            fl(128, 3 * WIDTH),
            fl(8, 128, 256),
            fl(4, 2, 128, 256),
            bf(4, 4, 128, 384),
            bf(128, WIDTH),
            bf(4, 8, 48, 128),
            bf(4, 48, 128),
            fl(160, 128),
            bf(8, WIDTH, 128),
            bf(8, 4, 16, WIDTH),
            bf(4, 128, 384),
            bf(8, 4, 16, 384),
            fl(3, 512, 128),
            fl(7, 512, 128),
            fl(3, 512, 128),
            bf(8, 4, 16, 384),
            bf(4, 8, 16, 384),
            bf(8, 16, WIDTH),
            bf(8, 16, WIDTH),
            fl(7, 512, 128),
            bf(512, 1024),
            bf(3, 8, 4, 16, CHUNK),
            bf(3, 3, 8, 16, CHUNK),
            bf(3, 8, 16, CHUNK),
            bf(3, 8, 16, CHUNK),
            bf(128, WIDTH),
            bf(8, WIDTH, 128),
            fl(4, 128, 128),
            bf(WIDTH, 128),
            bf(WIDTH, 128),
            bf(3, WIDTH, 128),
            bf(3, WIDTH, 128),
            bf(3, WIDTH, 128),
            bf(WIDTH, 128),
            bf(8, BLOCK, 128),
            fl(160, 128),
            bf(4, 48, 128),
            bf(4, 48, 128),
            bf(8, 4, 48, 128),
            fl(48, 3 * WIDTH),
            dma((2,)), dma((3,)), dma((3,)), dma((7,)), dma((7,)),
            dma((8, 3)), dma((8, 3)), dma((8,)), dma((8,)),
            dma((3,)), dma((3,)), dma((7,)), dma((7,)),
            dma((7,)), dma((7,)), dma((8, 3)), dma((8, 3)),
            dma((3,)), dma((3,)), dma((7,)), dma((7,)),
            dma((3, 3)), dma((3, 3)), dma((3, 7)), dma((3, 7)),
            dma, dma, dma, dma((3,)),
            dma((3,)), dma((3,)), dma((3, 3)), dma((3, 3)), dma((8,)), dma((8,)),
            dma((3,)), dma((3,)), dma((4, 8)), dma((8, 4)),
        ],
        compiler_params=pltpu.CompilerParams(
            collective_id=0, has_side_effects=True, vmem_limit_bytes=52 * 1024 * 1024
        ),
    )(
        lengths, spatial_qkv.reshape(patches, 3 * WIDTH), w_qkv,
        cotangent.reshape(patches, WIDTH),
    )
    return (
        out[0].reshape(1, frames, patches, WIDTH),
        out[1].reshape(1, frames, patches, 3 * WIDTH),
        out[2],
    )


def solution(mesh):
    in_specs = (P("dp", "seq", None, None), P("dp"), P("seq", None), P("dp", "seq", None, None))
    out_specs = (P("dp", "seq", None, None), P("dp", "seq", None, None), P("seq", "dp"))
    return jax.shard_map(local, mesh=mesh, in_specs=in_specs, out_specs=out_specs, check_vma=False)
```

```python
import jax
import jax.numpy as jnp
from jax import lax
from jax.experimental import pallas as pl
from jax.experimental.pallas import tpu as pltpu
from jax.sharding import PartitionSpec as P

HEADS = 16
WIDTH = 1152
HEAD = 72
NY, NZ, NX, NC = 4, 8, 4, 2
MESH = pl.DeviceIdType.MESH
F32, BF16 = jnp.float32, jnp.bfloat16
SCALE = HEAD ** (-0.5)


def dot(a, b):
    return lax.dot_general(a, b, (((1,), (0,)), ((), ())), preferred_element_type=F32)


def dot_nt(a, b):
    return lax.dot_general(a, b, (((1,), (1,)), ((), ())), preferred_element_type=F32)


def dot_tn(a, b):
    return lax.dot_general(a, b, (((0,), (0,)), ((), ())), preferred_element_type=F32)


def half(window, pair):
    return window[:, 0:256] if pair == 0 else window[:, 128:384]


def head_masks(off):
    lane = lax.broadcasted_iota(jnp.int32, (128, 256), 1)
    masks = []
    for j in range(4):
        low = off + HEAD * j - (128 if j >= 2 else 0)
        masks.append(jnp.where((lane >= low) & (lane < low + HEAD), 1.0, 0.0).astype(BF16))
    return masks


def two(window, pair, masks):
    own = half(window, pair)
    return jnp.concatenate([own * masks[2 * pair], own * masks[2 * pair + 1]], axis=0)


def stack(array):
    return jnp.concatenate([array[:, 0:128], array[:, 128:256]], axis=0)


def join(parts):
    left, right = parts
    return jnp.concatenate(
        [left[:, 0:128], left[:, 128:256] + right[:, 0:128], right[:, 128:256]], axis=1
    )


def forward4(q, k, v, masks, live):
    probs, outs = [], []
    for pair in range(2):
        scores = dot_nt(half(k, pair), two(q, pair, masks)) * SCALE
        if live is not None:
            scores = jnp.where(live, scores, -1e30)
        expo = jnp.exp(scores - jnp.max(scores, axis=0, keepdims=True))
        prob = expo * (1.0 / jnp.sum(expo, axis=0, keepdims=True))
        probs.append(prob)
        outs.append(dot_tn(stack(prob.astype(BF16)), two(v, pair, masks)))
    return join(outs), probs


def backward4(g, q, k, v, probs, masks, values=True):
    dqs, dks, dvs = [], [], []
    for pair in range(2):
        prob = probs[pair]
        g_two = two(g, pair, masks)
        if values:
            dvs.append(dot(prob.astype(BF16), g_two))
        gp = dot_nt(half(v, pair), g_two)
        gs = prob * (gp - jnp.sum(gp * prob, axis=0, keepdims=True))
        low = (gs * SCALE).astype(BF16)
        dqs.append(dot_tn(stack(low), two(k, pair, masks)))
        dks.append(dot(low, two(q, pair, masks)))
    return (join(dqs), join(dks)) + ((join(dvs),) if values else ())


def remote(src, dst, ssem, rsem, dp, s):
    return pltpu.make_async_remote_copy(
        src_ref=src, dst_ref=dst, send_sem=ssem, recv_sem=rsem,
        device_id=(dp, s), device_id_type=MESH,
    )


def m16(value):
    return pl.multiple_of(value, 16)


Z_ORDER = (1, 7, 2, 6, 3, 5, 4)
BLOCK = 144
CHUNK = 384


PART_AT = (2 * WIDTH, 0, WIDTH)
OWNER = (0, 6, 1, 2, 3, 4, 5, 7)


def placed(group, tile):
    found = set()
    for part in range(3):
        low = max(128 * tile, 288 * part)
        high = min(128 * tile + 128, 288 * part + 288)
        if low < high:
            shift = PART_AT[part] + 288 * group - 288 * part
            found |= set(range((low + shift) // 432, (high - 1 + shift) // 432 + 1))
    return sorted(found)


def tile_owner(tile):
    return 2 * (OWNER[tile] % 4) + OWNER[tile] // 4


def kernel(
    len_ref, qkv_h, w, cot_h, bo, gqkv, gw,
    qkv, cot, acc, prs, prt, blk, sob, wp, wr, wm, wf, so, cy, cz, c32, pj, to32, tob, ty, tw, tf,
    gp32, gpb, gs, gr, gz, gf, grad, pw, dv2, cre, kre, crv, kr, xr, zr, zb, fr, fs, fd, gwf,
    in_s, wy_s, wy_r, wz_s, wz_r, wx_s, wx_r, wd_s, wd_r, cy_s, cy_r, cz_s, cz_r,
    sz_s, sz_r, sy_s, sy_r, ty_s, ty_r, tz_s, tz_r, gy_s, gy_r, gz_s, gz_r,
    pe_s, pe_r, pxe_s, pxe_r, pc_s, pc_r, px_s, px_r, pz_s, pz_r, pd_s, pd_r,
):
    dp, s = lax.axis_index("dp"), lax.axis_index("seq")
    y, z = lax.rem(s, NY), lax.div(s, NY)
    c, x = lax.rem(dp, NC), lax.div(dp, NC)
    sib = x * NC + (1 - c)
    mine = 4 * c + x
    sent = []

    def at_y(k):
        return lax.rem(y + k + NY, NY)

    def at_z(k):
        return lax.rem(z + k + NZ, NZ)

    def at_x(k):
        return lax.rem(x + k + NX, NX)

    def send(src, dst, ssem, rsem, dp_to, s_to):
        copy = remote(src, dst, ssem, rsem, dp_to, s_to)
        copy.start()
        sent.append(copy)

    def arrived(dst, ssem, rsem):
        remote(dst, dst, ssem, rsem, dp, s).wait_recv()

    barrier = pltpu.get_barrier_semaphore()
    for k in range(1, NZ):
        pl.semaphore_signal(barrier, inc=1, device_id=(dp, at_z(k) * NY + y), device_id_type=MESH)
    for k in range(1, NX * NC * NY):
        to = (lax.rem(dp + k, NX * NC), z * NY + at_y(k // (NX * NC)))
        pl.semaphore_signal(barrier, inc=1, device_id=to, device_id_type=MESH)
    qkv_in = pltpu.make_async_copy(qkv_h, qkv, in_s.at[0])
    cot_in = pltpu.make_async_copy(cot_h, cot, in_s.at[1])
    qkv_in.start()
    cot_in.start()

    wrow = w[...].astype(F32)
    for g in range(NY):
        piece = jnp.concatenate(
            [wrow[:, 288 * g + at: 288 * g + at + 288] for at in PART_AT]
            + [jnp.zeros((36, 160), F32)], axis=1
        )
        piece = jnp.concatenate([piece, jnp.zeros((12, 1024), F32)], axis=0).astype(BF16)
        for t in range(8):
            wp[g, OWNER[t]] = piece[:, 128 * t: 128 * t + 128]
    wr[y] = wp[y, mine]

    def spatial_forward(group):
        at = pl.multiple_of(256 * group, 128)
        q, k, v = (qkv[:, pl.ds(at + WIDTH * i, 384)] for i in range(3))
        out, probs = forward4(q, k, v, head_masks(32 * group), None)
        acc[:, pl.ds(at, 384)] += out
        for j in range(2):
            prs[2 * group + j] = probs[j]


    pl.semaphore_wait(barrier, NZ + NX * NC * NY - 2)
    for k in range(1, NY):
        to = at_y(k)
        send(wp.at[to, mine], wr.at[y], wy_s.at[k - 1], wy_r.at[k - 1], dp, z * NY + to)
    acc[...] = jnp.zeros_like(acc)
    fd[...] = jnp.zeros_like(fd)
    cot_in.wait()
    cy[y] = cot[:, pl.ds(pl.multiple_of(256 * y, 128), 384)]
    for k in range(1, NY):
        to = at_y(k)
        send(
            cot.at[:, pl.ds(pl.multiple_of(256 * to, 128), 384)], cy.at[y],
            cy_s.at[k - 1], cy_r.at[k - 1], dp, z * NY + to,
        )

    qkv_in.wait()
    for group in range(4):
        spatial_forward(group)
    sob[...] = acc[:, 0:WIDTH].astype(BF16)
    so[z, y] = sob[pl.ds(m16(16 * z), 16), :]

    for k in range(1, NY):
        arrived(wr.at[at_y(-k)], wy_s.at[k - 1], wy_r.at[k - 1])
    for i in range(NY):
        wm[36 * i: 36 * i + 48, :] = wr[i].astype(F32)
    wf[mine, pl.ds(m16(BLOCK * z), BLOCK)] = wm[0:BLOCK, :].astype(BF16)

    def rows(k):
        return pl.ds(m16(BLOCK * at_z(k)), BLOCK)

    def weight_x(order, k):
        for i in range(1, NX):
            block = wf.at[mine, rows(k)]
            send(block, block, wx_s.at[order, i - 1], wx_r.at[order, i - 1], at_x(i) * NC + c, s)

    def spread_y(order, k):
        for i in range(1, NY):
            block = so.at[at_z(k), y]
            send(block, block, sy_s.at[order, i - 1], sy_r.at[order, i - 1], dp, z * NY + at_y(i))

    def weight_on(k, step, way):
        block = wf.at[mine, rows(k)]
        send(block, block, wz_s.at[way - 1], wz_r.at[way - 1], dp, at_z(step) * NY + y)

    for k in (1, 7, 2, 6):
        weight_on(0, k, k)
    weight_x(0, 0)
    for k in Z_ORDER:
        to = at_z(k)
        send(
            sob.at[pl.ds(m16(16 * to), 16)], so.at[z, y],
            sz_s.at[k - 1], sz_r.at[k - 1], dp, to * NY + y,
        )
    spread_y(0, 0)
    for order, k in enumerate(Z_ORDER):
        arrived(wf.at[mine, rows(-k)], wz_s.at[k - 1], wz_r.at[k - 1])
        if k == 2:
            weight_on(-2, 1, 3)
            weight_on(-2, 2, 4)
        if k == 6:
            weight_on(2, -1, 5)
        weight_x(order + 1, -k)
        arrived(so.at[at_z(-k), y], sz_s.at[k - 1], sz_r.at[k - 1])
        spread_y(order + 1, -k)

    for k in range(1, NY):
        arrived(cy.at[at_y(-k)], cy_s.at[k - 1], cy_r.at[k - 1])
    for k in Z_ORDER:
        to = at_z(k)
        send(
            cy.at[:, pl.ds(m16(16 * to), 16)], cz.at[z],
            cz_s.at[k - 1], cz_r.at[k - 1], dp, to * NY + y,
        )
    cz[z] = cy[:, pl.ds(m16(16 * z), 16), :]

    for order, k in enumerate((0,) + Z_ORDER):
        for i in range(1, NX):
            arrived(
                wf.at[4 * c + at_x(-i), rows(-k)], wx_s.at[order, i - 1], wx_r.at[order, i - 1]
            )
        block = wf.at[pl.ds(4 * c, 4), rows(-k)]
        send(block, block, wd_s.at[order], wd_r.at[order], sib, s)
    for order, k in enumerate((0,) + Z_ORDER):
        for i in range(1, NY):
            arrived(so.at[at_z(-k), at_y(-i)], sy_s.at[order, i - 1], sy_r.at[order, i - 1])
    for order, k in enumerate((0,) + Z_ORDER):
        arrived(wf.at[pl.ds(4 - 4 * c, 4), rows(-k)], wd_s.at[order], wd_r.at[order])

    every = so[...].reshape(512, WIDTH)
    for t in range(4):
        if t < 3:
            pair = dot(
                every, jnp.concatenate([wf[OWNER[2 * t]], wf[OWNER[2 * t + 1]]], axis=1)
            )
            pj[2 * t], pj[2 * t + 1] = pair[:, 0:128], pair[:, 128:256]
        else:
            pj[6] = dot(every, wf[OWNER[6]])

    length = len_ref[0]
    key = lax.broadcasted_iota(jnp.int32, (128, 256), 0)
    query = lax.broadcasted_iota(jnp.int32, (128, 256), 1) & 127
    live = ((key >> 5) == (query >> 5)) & ((key & 31) < length)
    masks = head_masks(0)

    def rows_of(ref, first, b):
        return jnp.concatenate(
            [
                jnp.concatenate(
                    [ref[t, pl.ds(4 * b + i, 32, stride=16), :] for i in range(4)], axis=0
                )
                for t in range(first, first + 3)
            ],
            axis=1,
        )

    def temporal_forward(b, carry):
        v = rows_of(pj, 0, b).astype(BF16)
        q = pltpu.roll(rows_of(pj, 2, b), 384 - 32, 1).astype(BF16)
        k = pltpu.roll(rows_of(pj, 4, b), 384 - 64, 1).astype(BF16)
        blk[b, 0], blk[b, 1], blk[b, 2] = q, k, v
        out, probs = forward4(q, k, v, masks, live)
        for j in range(2):
            prt[b, j] = probs[j]
        for i in range(4):
            for t in range(3):
                to32[t, pl.ds(4 * b + i, 32, stride=16), :] = out[
                    32 * i: 32 * i + 32, 128 * t: 128 * t + 128
                ]
        return carry

    for b in range(0, 4):
        temporal_forward(b, 0)

    t_out = jnp.concatenate([to32[t] for t in range(3)], axis=1)
    turned = t_out
    for k in range(1, NY):
        turned = jnp.where(y == k, pltpu.roll(t_out, 32 * k, 1), turned)
    tob[...] = turned.astype(BF16).reshape(NZ, NY, 16, 384)
    for k in range(1, NY):
        to = at_y(k)
        send(tob.at[:, to], ty.at[y], ty_s.at[k - 1], ty_r.at[k - 1], dp, z * NY + to)
    ty[y] = tob[:, y]

    for k in Z_ORDER:
        arrived(cz.at[at_z(-k)], cz_s.at[k - 1], cz_r.at[k - 1])
    g_in = cz[...].reshape(512, 384).astype(F32)
    turned = g_in
    for k in range(1, NY):
        turned = jnp.where(y == k, pltpu.roll(g_in, 384 - 32 * k, 1), turned)
    for t in range(3):
        c32[t] = turned[:, 128 * t: 128 * t + 128]

    def scatter(ref, first, b, array):
        for i in range(4):
            for t in range(array.shape[1] // 128):
                ref[first + t, pl.ds(4 * b + i, 32, stride=16), :] = array[
                    32 * i: 32 * i + 32, 128 * t: 128 * t + 128
                ]

    def temporal_values(b, carry):
        g = rows_of(c32, 0, b).astype(BF16)
        blk[b, 3] = g
        dv = join([
            dot(prt[b, pair].astype(BF16), two(g, pair, masks)) for pair in range(2)
        ])
        scatter(gp32, 0, b, dv[:, 0:256])
        dv2[b] = dv[:, 256:384]
        return carry

    def temporal_backward(b, carry):
        q, k, v, g = blk[b, 0], blk[b, 1], blk[b, 2], blk[b, 3]
        dq, dk = backward4(g, q, k, v, [prt[b, j] for j in range(2)], masks, False)
        dq, dk = pltpu.roll(dq, 32, 1), pltpu.roll(dk, 64, 1)
        packed = jnp.concatenate(
            [dv2[b] + dq[:, 0:128], dq[:, 128:256], dq[:, 256:384] + dk[:, 0:128], dk[:, 128:384]],
            axis=1,
        )
        scatter(gp32, 2, b, packed)
        return carry

    def weight_part(at, low, high):
        part = dot_tn(
            so[:, :, :, at: at + CHUNK].reshape(512, CHUNK), gpb[:, 128 * low: 128 * high]
        ).astype(BF16)
        for t in range(low, high):
            pw[OWNER[t], at: at + CHUNK] = part[:, 128 * (t - low): 128 * (t - low) + 128]

    early, late = x == 2 * c, (x != 2 * c) & (mine != 7)

    def early_weight():
        for i in range(3):
            weight_part(CHUNK * i, 0, 2)
        send(pw.at[6 - 6 * c], cre, pe_s, pe_r, sib, s)

    def early_to():
        k = lax.rem(2 * c - x + NX, NX)
        slot = jnp.maximum(k - 1, 0)
        return remote(
            kre, xr.at[slot], pxe_s, pxe_r.at[slot], 2 * c * NC + c, s
        )

    def early_sum():
        arrived(cre, pe_s, pe_r)
        kre[...] = (pw[6 * c].astype(F32) + cre[...].astype(F32)).astype(BF16)

        @pl.when(x != 2 * c)
        def _():
            early_to().start()

    for b in range(0, 4):
        temporal_values(b, 0)
    for t in range(2):
        gpb[:, 128 * t: 128 * t + 128] = gp32[t].astype(BF16)
    early_weight()
    for b in range(0, 2):
        temporal_backward(b, 0)
    early_sum()
    for b in range(2, 4):
        temporal_backward(b, 0)
    for t in range(2, 7):
        gpb[:, 128 * t: 128 * t + 128] = gp32[t].astype(BF16)

    def weight_chunk(i):
        at = CHUNK * i
        weight_part(at, 2, 7)
        send(
            pw.at[pl.ds(4 - 3 * c, 3), at: at + CHUNK], crv.at[:, at: at + CHUNK],
            pc_s.at[i], pc_r.at[i], sib, s,
        )

    def back_chunk(i):
        at = CHUNK * i
        part = jnp.zeros((512, CHUNK), F32)
        for t in range(4):
            if t < 3:
                weight = jnp.concatenate(
                    [wf[OWNER[2 * t], at: at + CHUNK], wf[OWNER[2 * t + 1], at: at + CHUNK]],
                    axis=1,
                )
                part = part + dot_nt(gpb[:, 256 * t: 256 * t + 256], weight)
            else:
                part = part + dot_nt(gpb[:, 768:896], wf[OWNER[6], at: at + CHUNK])
        gs[i] = part.astype(BF16).reshape(NZ, NY, 16, CHUNK)
        for k in range(1, NY):
            to = at_y(k)
            send(
                gs.at[i, :, to], gr.at[i, k - 1],
                gy_s.at[i, k - 1], gy_r.at[i, k - 1], dp, z * NY + to,
            )

    def late_to(i, k):
        at = CHUNK * i
        to = at_x(k)
        wanted = (to != 2 * c) & (4 * c + to != 7)
        return wanted, remote(
            kr.at[jnp.clip(to - 1 + c, 0, 2), at: at + CHUNK], xr.at[k - 1, at: at + CHUNK],
            px_s.at[i, k - 1], px_r.at[i, k - 1], to * NC + c, s,
        )

    def weight_sum(i):
        at = CHUNK * i
        arrived(crv.at[:, at: at + CHUNK], pc_s.at[i], pc_r.at[i])
        kr[:, at: at + CHUNK] = (
            pw[pl.ds(1 + 3 * c, 3), at: at + CHUNK].astype(F32)
            + crv[:, at: at + CHUNK].astype(F32)
        ).astype(BF16)
        for k in range(1, NX):
            wanted, copy = late_to(i, k)
            pl.when(wanted)(copy.start)

    def weight_z(i, blocks):
        at = CHUNK * i

        @pl.when(late)
        def _():
            for k in range(1, NX):
                arrived(xr.at[k - 1, at: at + CHUNK], px_s.at[i, k - 1], px_r.at[i, k - 1])

        if i == 0:
            @pl.when(early)
            def _():
                for k in range(1, NX):
                    arrived(xr.at[k - 1], pxe_s, pxe_r.at[k - 1])

        total = jnp.where(
            early, kre[at: at + CHUNK].astype(F32),
            kr[jnp.clip(x - 1 + c, 0, 2), at: at + CHUNK].astype(F32),
        )
        for k in range(1, NX):
            total = total + xr[k - 1, at: at + CHUNK].astype(F32)
        total = jnp.where(early | late, total, 0.0)
        zr[at: at + CHUNK] = total.astype(BF16)
        for b in blocks:
            @pl.when(z != b)
            def _():
                remote(
                    zr.at[BLOCK * b: BLOCK * b + BLOCK], zb.at[z],
                    pz_s.at[b], pz_r.at[z], dp, b * NY + y,
                ).start()

    def back_sum(i):
        for k in range(1, NY):
            arrived(gr.at[i, k - 1], gy_s.at[i, k - 1], gy_r.at[i, k - 1])
        total = gs[i, :, y].astype(F32)
        for k in range(1, NY):
            total = total + gr[i, k - 1].astype(F32)
        gz[i] = total.astype(BF16)
        for k in Z_ORDER:
            to = at_z(k)
            send(
                gz.at[i, to], gf.at[i, z], gz_s.at[i, k - 1], gz_r.at[i, k - 1], dp, to * NY + y
            )
        gf[i, z] = gz[i, z]

    def back_done(i):
        at = CHUNK * i
        for k in Z_ORDER:
            arrived(gf.at[i, at_z(-k)], gz_s.at[i, k - 1], gz_r.at[i, k - 1])
        grad[:, at: at + CHUNK] = (
            cot[:, at: at + CHUNK].astype(F32) + gf[i].reshape(128, CHUNK).astype(F32)
        ).astype(BF16)

    def spatial_backward(group):
        at = 256 * group
        q, k, v = (qkv[:, at + WIDTH * i: at + WIDTH * i + 384] for i in range(3))
        probs = [prs[2 * group + j] for j in range(2)]
        grads = backward4(grad[:, at: at + 384], q, k, v, probs, head_masks(32 * group))
        for i in range(3):
            acc[:, at + WIDTH * i: at + WIDTH * i + 384] += grads[i]

    def out_z():
        for k in range(1, NY):
            arrived(ty.at[at_y(-k)], ty_s.at[k - 1], ty_r.at[k - 1])
        whole = [None] * 9
        for i in range(NY):
            for t in range(3):
                tile = ty[i, :, :, 128 * t: 128 * t + 128].astype(F32)
                at = 2 * i + t
                whole[at] = tile if whole[at] is None else whole[at] + tile
        for t in range(9):
            tw[:, :, 128 * t: 128 * t + 128] = whole[t].astype(BF16)
        for k in Z_ORDER:
            to = at_z(k)
            send(tw.at[to], tf.at[z], tz_s.at[k - 1], tz_r.at[k - 1], dp, to * NY + y)
        tf[z] = tw[z]

    def final_y():
        zb[z] = zr[pl.ds(m16(BLOCK * z), BLOCK)]
        for b in range(NZ):
            @pl.when(z != b)
            def _():
                arrived(zb.at[b], pz_s.at[b], pz_r.at[b])
        total = zb[0].astype(F32)
        for i in range(1, NZ):
            total = total + zb[i].astype(F32)
        fr[0:BLOCK, :] = total
        fr[BLOCK:160, :] = jnp.zeros((16, 128), F32)
        for i in range(NY):
            fs[i] = fr[36 * i: 36 * i + 48, :].astype(BF16)
        each_move(lambda copy: copy.start())
        fd[mine, y] = fs[y]

    def each_move(act):
        for tile in range(7):
            for g in range(NY):
                @pl.when((mine == OWNER[tile]) & (y == g))
                def _():
                    for d in placed(g, tile):
                        for k in range(1 if d == tile_owner(tile) else 0, NY):
                            act(remote(
                                fs.at[at_y(k)], fd.at[OWNER[tile], g],
                                pd_s.at[k, d], pd_r.at[tile, g], d, z * NY + at_y(k),
                            ))

    weight_chunk(0)
    back_chunk(0)
    weight_chunk(1)
    weight_sum(0)
    out_z()
    weight_chunk(2)
    weight_sum(1)
    back_chunk(1)
    weight_sum(2)
    back_chunk(2)
    acc[...] = jnp.zeros_like(acc)
    weight_z(0, (0, 1))
    back_sum(0)
    weight_z(1, (2, 3, 4))
    back_sum(1)
    weight_z(2, (5, 6, 7))
    back_sum(2)
    back_done(0)
    spatial_backward(0)
    final_y()
    back_done(1)
    spatial_backward(1)
    back_done(2)
    spatial_backward(2)
    spatial_backward(3)
    gqkv[...] = acc[...].astype(BF16)
    for k in Z_ORDER:
        arrived(tf.at[at_z(-k)], tz_s.at[k - 1], tz_r.at[k - 1])
    bo[...] = (sob[...].astype(F32) + tf[...].reshape(128, WIDTH).astype(F32)).astype(BF16)

    for d in range(NX * NC):
        @pl.when(dp == d)
        def _():
            for tile in range(7):
                for g in range(NY):
                    if d not in placed(g, tile):
                        continue
                    copy = remote(
                        fd.at[OWNER[tile], g], fd.at[OWNER[tile], g],
                        pd_s.at[0, d], pd_r.at[tile, g], d, s,
                    )
                    if d == tile_owner(tile):
                        pl.when(y != g)(copy.wait_recv)
                    else:
                        copy.wait_recv()
    gwf[...] = jnp.zeros_like(gwf)
    lane = lax.broadcasted_iota(jnp.int32, (48, 384), 1)
    for g in range(NY):
        for i in range(3):
            window = jnp.concatenate(
                [fd[OWNER[2 * i + t], g].astype(F32) for t in range(3)], axis=1
            )
            if i > 0:
                window = pltpu.roll(window, 384 - 32 * i, 1)
            window = jnp.where(lane < 288, window, 0.0)
            if g > 0:
                window = pltpu.roll(window, 32 * g, 1)
            at = PART_AT[i] + 256 * g
            gwf[:, at: at + 384] += window
    picked = jnp.zeros((48, 432), F32)
    for d in range(NX * NC):
        picked = jnp.where(dp == d, gwf[:, 432 * d: 432 * d + 432], picked)
    gw[...] = picked[0:36].astype(BF16)

    for copy in sent:
        copy.wait_send()

    @pl.when(x != 2 * c)
    def _():
        early_to().wait_send()

    for i in range(3):
        for k in range(1, NX):
            wanted, copy = late_to(i, k)
            pl.when(wanted)(copy.wait_send)
    for b in range(NZ):
        @pl.when(z != b)
        def _():
            remote(
                zr.at[BLOCK * b: BLOCK * b + BLOCK], zb.at[z], pz_s.at[b], pz_r.at[z], dp, s
            ).wait_send()
    each_move(lambda copy: copy.wait_send())


def local(spatial_qkv, lengths, w_qkv, cotangent):
    frames, patches = spatial_qkv.shape[1], spatial_qkv.shape[2]
    vmem = pl.BlockSpec(memory_space=pltpu.VMEM)
    hbm = pl.BlockSpec(memory_space=pltpu.HBM)
    dma = pltpu.SemaphoreType.DMA

    def bf(*shape):
        return pltpu.VMEM(shape, BF16)

    def fl(*shape):
        return pltpu.VMEM(shape, F32)

    out = pl.pallas_call(
        kernel,
        out_shape=(
            jax.ShapeDtypeStruct((patches, WIDTH), BF16),
            jax.ShapeDtypeStruct((patches, 3 * WIDTH), BF16),
            jax.ShapeDtypeStruct((36, 432), BF16),
        ),
        in_specs=[pl.BlockSpec(memory_space=pltpu.SMEM), hbm, vmem, hbm],
        out_specs=(vmem, vmem, vmem),
        scratch_shapes=[
            bf(128, 3 * WIDTH),
            bf(128, WIDTH),
            fl(128, 3 * WIDTH),
            fl(8, 128, 256),
            fl(4, 2, 128, 256),
            bf(4, 4, 128, 384),
            bf(128, WIDTH),
            bf(4, 8, 48, 128),
            bf(4, 48, 128),
            fl(160, 128),
            bf(8, WIDTH, 128),
            bf(8, 4, 16, WIDTH),
            bf(4, 128, 384),
            bf(8, 4, 16, 384),
            fl(3, 512, 128),
            fl(7, 512, 128),
            fl(3, 512, 128),
            bf(8, 4, 16, 384),
            bf(4, 8, 16, 384),
            bf(8, 16, WIDTH),
            bf(8, 16, WIDTH),
            fl(7, 512, 128),
            bf(512, 1024),
            bf(3, 8, 4, 16, CHUNK),
            bf(3, 3, 8, 16, CHUNK),
            bf(3, 8, 16, CHUNK),
            bf(3, 8, 16, CHUNK),
            bf(128, WIDTH),
            bf(8, WIDTH, 128),
            fl(4, 128, 128),
            bf(WIDTH, 128),
            bf(WIDTH, 128),
            bf(3, WIDTH, 128),
            bf(3, WIDTH, 128),
            bf(3, WIDTH, 128),
            bf(WIDTH, 128),
            bf(8, BLOCK, 128),
            fl(160, 128),
            bf(4, 48, 128),
            bf(8, 4, 48, 128),
            fl(48, 3 * WIDTH),
            dma((2,)), dma((3,)), dma((3,)), dma((7,)), dma((7,)),
            dma((8, 3)), dma((8, 3)), dma((8,)), dma((8,)),
            dma((3,)), dma((3,)), dma((7,)), dma((7,)),
            dma((7,)), dma((7,)), dma((8, 3)), dma((8, 3)),
            dma((3,)), dma((3,)), dma((7,)), dma((7,)),
            dma((3, 3)), dma((3, 3)), dma((3, 7)), dma((3, 7)),
            dma, dma, dma, dma((3,)),
            dma((3,)), dma((3,)), dma((3, 3)), dma((3, 3)), dma((8,)), dma((8,)),
            dma((4, 8)), dma((8, 4)),
        ],
        compiler_params=pltpu.CompilerParams(
            collective_id=0, has_side_effects=True, vmem_limit_bytes=52 * 1024 * 1024
        ),
    )(
        lengths, spatial_qkv.reshape(patches, 3 * WIDTH), w_qkv,
        cotangent.reshape(patches, WIDTH),
    )
    return (
        out[0].reshape(1, frames, patches, WIDTH),
        out[1].reshape(1, frames, patches, 3 * WIDTH),
        out[2],
    )


def solution(mesh):
    in_specs = (P("dp", "seq", None, None), P("dp"), P("seq", None), P("dp", "seq", None, None))
    out_specs = (P("dp", "seq", None, None), P("dp", "seq", None, None), P("seq", "dp"))
    return jax.shard_map(local, mesh=mesh, in_specs=in_specs, out_specs=out_specs, check_vma=False)
```
